32 devices in a mesh: blk: 8 (over z, x), head: 4 (over y, core).
Axes of the slice: x: 2, y: 2, z: 4, core: 2. Of those that a mesh axis runs over, the one named last changes fastest.
Arguments:
- tokens: bfloat16 [6144, 2048], P(('blk', 'head')), may hold values from -6 to 6
- attn_gain: bfloat16 [2048], P('blk'), may hold values from 0.25 to 1.75
- query_weight: bfloat16 [2048, 2048], P('blk', 'head'), may hold values from -0.125 to 0.125
- key_matrix: bfloat16 [2048, 1024], P('blk', 'head'), may hold values from -0.125 to 0.125
- value_matrix: bfloat16 [2048, 1024], P('blk', 'head'), may hold values from -0.125 to 0.125
- out_weight: bfloat16 [2048, 2048], P('head', 'blk'), may hold values from -3 to 3
- mlp_gain: bfloat16 [2048], P('blk'), may hold values from 0.25 to 1.75
- gate_weight: bfloat16 [2048, 8192], P('blk', 'head'), may hold values from -0.125 to 0.125
- up_weight: bfloat16 [2048, 8192], P('blk', 'head'), may hold values from -0.125 to 0.125
- down_weight: bfloat16 [8192, 2048], P('head', 'blk'), may hold values from -0.0625 to 0.0625
- segment_ids: int32 [6144], replicated, may hold values from 0 to 7, as said below
- positions: int32 [6144], replicated, may hold values from 0 to 8190, as said below
- cotangent: bfloat16 [6144, 2048], P(('blk', 'head')), may hold values from -6 to 6
Outputs:
- layer_out: bfloat16 [6144, 2048], P(('blk', 'head'))
- tokens_grad: float32 [6144, 2048], P(('blk', 'head'))
- attn_gain_grad: float32 [2048], P('blk')
- query_grad: float32 [2048, 2048], P('blk', 'head')
- key_grad: float32 [2048, 1024], P('blk', 'head')
- value_grad: float32 [2048, 1024], P('blk', 'head')
- out_grad: float32 [2048, 2048], P('head', 'blk')
- mlp_gain_grad: float32 [2048], P('blk')
- gate_grad: float32 [2048, 8192], P('blk', 'head')
- up_grad: float32 [2048, 8192], P('blk', 'head')
- down_grad: float32 [8192, 2048], P('head', 'blk')
The draws below stay inside these ranges and needn't reach their ends.
Inputs may be any that keep to these rules, and one draw needn't show every extreme that they name: `segment_ids`: document number of each token of the stream, never falling along it; a document holds 1 to 4096 tokens and one holds exactly 4096; the first document is numbered 0 and the last one carries the largest number. Within a document the positions rise by one from token to token; the first token of the stream has position 0.
All inputs are finite; a program needn't handle non-finite values.
Results may differ from the reference program's by a relative error of at most 0.02.
Values may be sent and summed in bfloat16 or wider, within the bound.
No kernel may reach another device: no remote copies, remote signals or barrier semaphores. Data moves between devices by JAX's collectives and lax.ppermute only.
A program may use at most 320 MiB of HBM per device.

```python
import math
import jax
import jax.numpy as jnp
from jax import lax

MODEL_WIDTH = 2048
FF = 8192
QUERY_HEADS_ALL = 8
KEY_VALUE_HEADS = 4
HEAD_WIDTH = 256
TOK_DEV = 192
SEQ = 4096
STREAM_TOKENS = 6144
QDIM = 2048
CYCLE = 6
N_HEAD = 4


def document_table(key):
    doc_count = STREAM_TOKENS // (SEQ // 4) + 2
    length_key, first_key, offset_key = jax.random.split(key, 3)
    lengths = jax.random.randint(length_key, (doc_count,), SEQ // 4, SEQ + 1)
    first_len = jax.random.randint(first_key, (), 1, min(SEQ, STREAM_TOKENS - SEQ) + 1)
    lengths = lengths.at[0].set(first_len).at[1].set(SEQ)
    starts = jnp.cumsum(lengths) - lengths
    offsets = jax.random.randint(offset_key, (doc_count,), 0, SEQ).at[0].set(0).at[1].set(SEQ - 1)
    token_index = jnp.arange(STREAM_TOKENS, dtype=jnp.int32)
    member = starts[None, :] <= token_index[:, None]
    segment = jnp.sum(member.astype(jnp.int32), axis=1) - 1
    chosen = segment[:, None] == jnp.arange(doc_count, dtype=jnp.int32)[None, :]
    doc_start = jnp.sum(jnp.where(chosen, starts[None, :], 0), axis=1)
    doc_offset = jnp.sum(jnp.where(chosen, offsets[None, :], 0), axis=1)
    last_doc = segment[STREAM_TOKENS - 1]
    numbered = jnp.where(segment == last_doc, STREAM_TOKENS // (SEQ // 4) + 1, segment)
    return (numbered.astype(jnp.int32), (token_index - doc_start + doc_offset).astype(jnp.int32))


def draw_segment_ids(key, part):
    return document_table(key)[0]


def draw_positions(key, part):
    return document_table(key)[1]


def spiked(values, key, source, target, shards_of, factor):
    owner, partner = [(jnp.arange(values.shape[axis_at]) // (values.shape[axis_at] // shards_of)).reshape([-1 if axis == axis_at else 1 for axis in range(values.ndim)]) for axis_at in (source, target)]
    chosen = jax.random.permutation(key, shards_of)[partner]
    strong = (owner == chosen) | (owner == (partner + shards_of // 2) % shards_of)
    return jnp.where(strong, factor * values, values)


def shard_levels(stream_key, shape, shards, least, largest):
    def one(dim, parts):
        draws = jax.random.uniform(jax.random.fold_in(jax.random.fold_in(stream_key, 6), dim), (parts,), jnp.float32, least / len(shards), largest / len(shards))
        return jnp.repeat(jnp.exp(draws), shape[dim] // parts).reshape((-1,) + (1,) * (len(shape) - dim - 1))

    level = one(*shards[0])
    for cut in shards[1:]:
        level = level * one(*cut)
    return level


def centred(own_key, extent, spread, most, cuts=(), kind=jnp.bfloat16):
    drawn = spread * jax.random.normal(own_key, extent, jnp.float32)
    if cuts:
        drawn = drawn * shard_levels(own_key, extent, cuts, -0.22, 0.18)
    return jnp.clip(drawn, -most, most).astype(kind)


def heavy_noise(own_key, shape, deviation, most, shards, heavy, held_as=jnp.bfloat16):
    result = deviation * jax.random.normal(own_key, shape, jnp.float32)
    if shards:
        result = result * shard_levels(own_key, shape, shards, -0.22, 0.18)
    return jnp.clip(spiked(result, jax.random.fold_in(own_key, 3), *heavy), -most, most).astype(held_as)


def setup_inputs(seed: int = 0) -> dict:
    keys = jax.random.split(jax.random.key(seed), 14)
    tokens = centred(keys[0], (STREAM_TOKENS, MODEL_WIDTH), 1.0, 6.0, ((0, 32),))
    attn_gain = jnp.clip(1.0 + 0.15 * jax.random.normal(keys[1], (MODEL_WIDTH,), jnp.float32), 0.25, 1.75).astype(jnp.bfloat16)
    query_weight = centred(keys[2], (MODEL_WIDTH, QDIM), MODEL_WIDTH ** -0.5, 0.125, ((0, 8), (1, 4)))
    key_matrix = centred(keys[3], (MODEL_WIDTH, KEY_VALUE_HEADS * HEAD_WIDTH), MODEL_WIDTH ** -0.5, 0.125, ((0, 8), (1, 4)))
    value_matrix = centred(keys[4], (MODEL_WIDTH, KEY_VALUE_HEADS * HEAD_WIDTH), MODEL_WIDTH ** -0.5, 0.125, ((0, 8), (1, 4)))
    out_weight = centred(keys[5], (QDIM, MODEL_WIDTH), (max(QDIM // 512, 1)) ** -0.5, 3.0, ((0, 4), (1, 8)))
    mlp_gain = jnp.clip(1.0 + 0.15 * jax.random.normal(keys[6], (MODEL_WIDTH,), jnp.float32), 0.25, 1.75).astype(jnp.bfloat16)
    gate_weight = centred(keys[7], (MODEL_WIDTH, FF), MODEL_WIDTH ** -0.5, 0.125, ((0, 8), (1, 4)))
    up_weight = centred(keys[8], (MODEL_WIDTH, FF), MODEL_WIDTH ** -0.5, 0.125, ((0, 8), (1, 4)))
    down_weight = centred(keys[9], (FF, MODEL_WIDTH), FF ** -0.5, 0.0625, ((0, 4), (1, 8)))
    segment_ids = draw_segment_ids(jax.random.fold_in(keys[13], 71), 0)
    positions = draw_positions(jax.random.fold_in(keys[13], 71), 0)
    cotangent = heavy_noise(keys[12], (STREAM_TOKENS, MODEL_WIDTH), 1.0, 6.0, ((0, 32),), (0, 1, 32, 2.75))
    return dict(tokens=tokens, attn_gain=attn_gain, query_weight=query_weight, key_matrix=key_matrix, value_matrix=value_matrix, out_weight=out_weight, mlp_gain=mlp_gain, gate_weight=gate_weight, up_weight=up_weight, down_weight=down_weight, segment_ids=segment_ids, positions=positions, cotangent=cotangent)


EPSILON = 1e-06
THETA_BASE = 1000042.0
MASKED = -1e+30

@jax.custom_vjp
def reduced_precision(v):
    return lax.optimization_barrier(v.astype(jnp.bfloat16)).astype(jnp.float32)

@jax.custom_vjp
def reduced_backward(v):
    return v

def low_keep(v):
    return (reduced_precision(v), None)

def low_pass(kept, grad):
    return (grad,)

def back_keep(v):
    return (v, None)

def back_low(kept, grad):
    return (reduced_precision(grad),)
reduced_precision.defvjp(low_keep, low_pass)
reduced_backward.defvjp(back_keep, back_low)

def norm_rows(values, gain_vec):
    inverse = lax.rsqrt(lax.optimization_barrier(jnp.mean(values * values, axis=-1, keepdims=True)) + EPSILON)
    return values * inverse * gain_vec

def apply_rotary(values, token_pos, direction):
    half_size = values.shape[-1] // 2
    frequency = THETA_BASE ** (-2.0 * jnp.arange(half_size, dtype=jnp.float32) / values.shape[-1])
    angles = token_pos.astype(jnp.float32)[:, None] * frequency[None, :]
    cosine = jnp.cos(angles)[:, None, :]
    sine_part = jnp.sin(angles)[:, None, :] * direction
    first_half = values[..., :half_size]
    second_half = values[..., half_size:]
    return jnp.concatenate([first_half * cosine - second_half * sine_part, second_half * cosine + first_half * sine_part], axis=-1)

def attend(query_rows, key_rot, value_linear, segment_ids):
    highest_precision = lax.Precision.HIGHEST
    rows_per_block = N_HEAD * TOK_DEV
    padding = CYCLE * rows_per_block
    window = padding + rows_per_block
    repetition_count = QUERY_HEADS_ALL // KEY_VALUE_HEADS
    score_scale = 1.0 / math.sqrt(HEAD_WIDTH)
    keys_pad = jnp.pad(key_rot, ((padding, 0), (0, 0), (0, 0)))
    values_pad = jnp.pad(value_linear, ((padding, 0), (0, 0), (0, 0)))
    segs_pad = jnp.pad(segment_ids, (padding, 0), constant_values=-1)
    blocks_of_query = query_rows.reshape(STREAM_TOKENS // rows_per_block, rows_per_block, KEY_VALUE_HEADS, repetition_count, HEAD_WIDTH)
    starts = jnp.arange(STREAM_TOKENS // rows_per_block, dtype=jnp.int32) * rows_per_block

    def one_block(inputs):
        query_block, block_start = inputs
        key_block = lax.dynamic_slice_in_dim(keys_pad, block_start, window, 0)
        value_block = lax.dynamic_slice_in_dim(values_pad, block_start, window, 0)
        key_segs = lax.dynamic_slice_in_dim(segs_pad, block_start, window, 0)
        query_segs = lax.dynamic_slice_in_dim(segment_ids, block_start, rows_per_block, 0)
        query_index = jnp.arange(rows_per_block, dtype=jnp.int32)[:, None] + padding
        key_index = jnp.arange(window, dtype=jnp.int32)[None, :]
        allowed = (query_segs[:, None] == key_segs[None, :]) & (key_index <= query_index)
        scores = jnp.einsum('qgrd,kgd->grqk', query_block, key_block, precision=highest_precision) * score_scale
        scores = jnp.where(allowed[None, None], reduced_backward(scores), MASKED)
        softmax_out = jax.nn.softmax(scores, axis=-1)
        mixed_values = jnp.einsum('grqk,kgd->qgrd', reduced_precision(softmax_out), value_block, precision=highest_precision)
        return mixed_values.reshape(rows_per_block, QUERY_HEADS_ALL * HEAD_WIDTH)
    return lax.map(jax.checkpoint(one_block), (blocks_of_query, starts)).reshape(STREAM_TOKENS, QUERY_HEADS_ALL * HEAD_WIDTH)

def forward(tokens, attn_gain, query_weight, key_matrix, value_matrix, out_weight, mlp_gain, gate_weight, up_weight, down_weight, segment_ids, positions):
    highest_precision = lax.Precision.HIGHEST
    normalized_input = reduced_precision(norm_rows(tokens, attn_gain))
    query_linear = reduced_backward(jnp.dot(normalized_input, query_weight, precision=highest_precision)).reshape(STREAM_TOKENS, QUERY_HEADS_ALL, HEAD_WIDTH)
    key_linear = reduced_backward(jnp.dot(normalized_input, key_matrix, precision=highest_precision)).reshape(STREAM_TOKENS, KEY_VALUE_HEADS, HEAD_WIDTH)
    value_linear = reduced_precision(reduced_backward(jnp.dot(normalized_input, value_matrix, precision=highest_precision))).reshape(STREAM_TOKENS, KEY_VALUE_HEADS, HEAD_WIDTH)
    query_rows = reduced_precision(apply_rotary(query_linear, positions, 1.0)).reshape(STREAM_TOKENS, KEY_VALUE_HEADS, QUERY_HEADS_ALL // KEY_VALUE_HEADS, HEAD_WIDTH)
    key_rot = reduced_precision(apply_rotary(key_linear, positions, 1.0))
    attn_full = attend(query_rows, key_rot, value_linear, segment_ids)
    attn_low = reduced_precision(reduced_backward(attn_full))
    branch = reduced_backward(jnp.dot(attn_low, out_weight, precision=highest_precision))
    residual = tokens + branch
    normed_mlp = reduced_precision(norm_rows(residual, mlp_gain))
    gate_lin = reduced_backward(jnp.dot(normed_mlp, gate_weight, precision=highest_precision))
    up_lin = reduced_backward(jnp.dot(normed_mlp, up_weight, precision=highest_precision))
    hidden = reduced_precision(jax.nn.silu(gate_lin) * up_lin)
    return residual + jnp.dot(hidden, down_weight, precision=highest_precision)

def reference(tokens, attn_gain, query_weight, key_matrix, value_matrix, out_weight, mlp_gain, gate_weight, up_weight, down_weight, segment_ids, positions, cotangent):
    primals = tuple((member.astype(jnp.float32) for member in (tokens, attn_gain, query_weight, key_matrix, value_matrix, out_weight, mlp_gain, gate_weight, up_weight, down_weight)))

    def closed(*entries):
        return forward(*entries, segment_ids, positions)
    output, pullback = jax.vjp(closed, *primals)
    gradients = pullback(cotangent.astype(jnp.float32))
    return (output.astype(jnp.bfloat16), gradients[0], gradients[1], gradients[2], gradients[3], gradients[4], gradients[5], gradients[6], gradients[7], gradients[8], gradients[9])
```

```python
import math

import jax
import jax.numpy as jnp
from jax import lax
from jax.sharding import PartitionSpec as P

QUERY_HEADS_ALL = 8
KEY_VALUE_HEADS = 4
HEAD_WIDTH = 256
SEQ = 4096

EPSILON = 1e-06
THETA_BASE = 1000042.0
MASKED = -1e30
BF = jnp.bfloat16
F32 = jnp.float32


def after(value, *deps):
    return lax.optimization_barrier((value, *deps))[0]


def cycle_order(count):
    return list(range(0, count, 2)) + list(range(count - 1, 0, -2))


def cycle_place(index, count):
    return jnp.where(index % 2 == 0, index // 2, count // 2 + (count - 1 - index) // 2)


def cycle_owner(place, count):
    place = lax.rem(place + 2 * count, count)
    return jnp.where(place < count // 2, 2 * place, 2 * (count - 1 - place) + 1)


def ring_routes(count):
    order = cycle_order(count)
    up = [(order[i], order[(i + 1) % count]) for i in range(count)]
    return up, [(b, a) for a, b in up]


def ring_gather(shard):
    count = lax.axis_size("blk")
    me = lax.axis_index("blk")
    place = cycle_place(me, count)
    up, down = ring_routes(count)
    rows = shard.shape[0]
    half = rows // 2
    out = jnp.zeros((count * rows, *shard.shape[1:]), shard.dtype)
    out = lax.dynamic_update_slice_in_dim(out, shard, me * rows, 0)
    left, right = shard, shard
    steps = []
    for step in range(1, count // 2 + 1):
        if step < count // 2:
            left = lax.ppermute(left, "blk", up)
            right = lax.ppermute(right, "blk", down)
            low, high = cycle_owner(place - step, count), cycle_owner(place + step, count)
            out = lax.dynamic_update_slice_in_dim(out, left, low * rows, 0)
            out = lax.dynamic_update_slice_in_dim(out, right, high * rows, 0)
        else:
            left = lax.ppermute(left[:half], "blk", up)
            right = lax.ppermute(right[half:], "blk", down)
            far = cycle_owner(place - step, count)
            out = lax.dynamic_update_slice_in_dim(out, left, far * rows, 0)
            out = lax.dynamic_update_slice_in_dim(out, right, far * rows + half, 0)
        steps.append((left, right))
    return out, steps


def ring_sum(blocks):
    count = lax.axis_size("blk")
    me = lax.axis_index("blk")
    place = cycle_place(me, count)
    up, down = ring_routes(count)
    rows = blocks.shape[0] // count
    half = rows // 2

    def part(offset):
        return lax.dynamic_slice_in_dim(
            blocks, cycle_owner(place + offset, count) * rows, rows, 0
        )

    far = part(count // 2)
    left = lax.ppermute(far[:half], "blk", up)
    right = lax.ppermute(far[half:], "blk", down)
    for step in range(count // 2 - 1, -1, -1):
        if step == count // 2 - 1:
            low, high = part(step), part(-step)
            left = jnp.concatenate([(low[:half].astype(F32) + left.astype(F32)).astype(BF), low[half:]])
            right = jnp.concatenate([high[:half], (high[half:].astype(F32) + right.astype(F32)).astype(BF)])
        elif step > 0:
            left = (part(step).astype(F32) + left.astype(F32)).astype(BF)
            right = (part(-step).astype(F32) + right.astype(F32)).astype(BF)
        else:
            return part(0).astype(F32) + left.astype(F32) + right.astype(F32)
        left = lax.ppermute(left, "blk", up)
        right = lax.ppermute(right, "blk", down)


def flip(value, axis, bit):
    return lax.ppermute(value, axis, [(i, i ^ bit) for i in range(lax.axis_size(axis))])


def head_gather(rows):
    other = flip(rows, "head", 2)
    pair = jnp.concatenate([rows, other], axis=0)
    beside = flip(pair, "head", 1)
    count = rows.shape[0]
    return jnp.concatenate([rows, beside[:count], other, beside[count:]], axis=0)


def head_sum(partial):
    low = partial.astype(BF).reshape(2, 2, partial.shape[0] // 4, *partial.shape[1:])
    near = flip(low[:, 1], "head", 1)
    pair = low[:, 0].astype(F32) + near.astype(F32)
    far = flip(pair[1].astype(BF), "head", 2)
    return pair[0] + far.astype(F32)


def slots(values, head_index):
    values = values.reshape(values.shape[0], 2, 2, values.shape[-1])
    values = jnp.where(head_index % 2 == 1, values[:, :, ::-1], values)
    values = jnp.where(head_index // 2 == 1, values[:, ::-1], values)
    return values.reshape(values.shape[0], -1)


def gain_gather(gains):
    count = lax.axis_size("blk")
    me = lax.axis_index("blk")
    bit = 1
    while bit < count:
        other = flip(gains, "blk", bit)
        low = jnp.concatenate([gains, other], axis=1)
        high = jnp.concatenate([other, gains], axis=1)
        gains = jnp.where((me // bit) % 2 == 0, low, high)
        bit *= 2
    return gains


def gain_sum(grad):
    for bit in (1, 2):
        grad = grad + flip(grad, "head", bit)
    count = lax.axis_size("blk")
    me = lax.axis_index("blk")
    bit = count // 2
    while bit:
        size = grad.shape[0] // 2
        upper = (me // bit) % 2 == 1
        keep = jnp.where(upper, grad[size:], grad[:size])
        send = jnp.where(upper, grad[:size], grad[size:])
        grad = keep + flip(send, "blk", bit)
        bit //= 2
    return grad


def rotary_table(token_pos, width):
    half_size = width // 2
    frequency = THETA_BASE ** (-2.0 * jnp.arange(half_size, dtype=F32) / width)
    angles = token_pos.astype(F32)[:, None] * frequency[None, :]
    return jnp.cos(angles)[:, None, :], jnp.sin(angles)[:, None, :]


def apply_rotary(values, table, direction):
    cosine, sine_part = table
    sine_part = sine_part * direction
    half_size = values.shape[-1] // 2
    first_half = values[..., :half_size]
    second_half = values[..., half_size:]
    return jnp.concatenate(
        [
            first_half * cosine - second_half * sine_part,
            second_half * cosine + first_half * sine_part,
        ],
        axis=-1,
    )


def norm_scale(values):
    return lax.rsqrt(jnp.mean(values * values, axis=-1, keepdims=True) + EPSILON)


def norm_back(values, gain_vec, inverse, upstream):
    weighted = upstream * gain_vec
    inner_mean = jnp.mean(weighted * values, axis=-1, keepdims=True)
    return inverse * weighted - values * (inverse * inverse * inverse) * inner_mean


def simple_product(matrix_a, matrix_b):
    return jnp.dot(matrix_a, matrix_b, preferred_element_type=F32)


def outer_sum(matrix_a, matrix_b):
    return lax.dot_general(
        matrix_a, matrix_b, (((0,), (0,)), ((), ())), preferred_element_type=F32
    )


def times_rows(matrix_a, matrix_b):
    return lax.dot_general(
        matrix_a, matrix_b, (((1,), (1,)), ((), ())), preferred_element_type=F32
    )


def block_scores(queries, key_part, allowed):
    score_scale = 1.0 / math.sqrt(queries.shape[-1])
    raw = jnp.einsum("qrd,kd->rqk", queries, key_part, preferred_element_type=F32) * score_scale
    return jnp.where(allowed[None], raw, MASKED)


def local(
    tokens,
    attn_gain,
    query_weight,
    key_matrix,
    value_matrix,
    out_weight,
    mlp_gain,
    gate_weight,
    up_weight,
    down_weight,
    segment_ids,
    positions,
    cotangent,
):
    heads = lax.axis_size("head")
    blocks = lax.axis_size("blk")
    blk = lax.axis_index("blk")
    head = lax.axis_index("head")
    own_rows = tokens.shape[0]
    rows = own_rows * heads
    window = min((SEQ + rows - 2) // rows + 1, blocks)
    width = HEAD_WIDTH
    repeats = QUERY_HEADS_ALL // KEY_VALUE_HEADS
    query_cols = query_weight.shape[1]

    segs = slots(segment_ids.reshape(blocks, heads, own_rows), head)
    poss = slots(positions.reshape(blocks, heads, own_rows), head)
    index = slots(jnp.arange(blocks * rows, dtype=jnp.int32).reshape(blocks, heads, own_rows), head)
    own_seg = lax.dynamic_index_in_dim(segs, blk, 0, False)
    own_pos = lax.dynamic_index_in_dim(poss, blk, 0, False)
    own_index = lax.dynamic_index_in_dim(index, blk, 0, False)
    first = jnp.maximum(blk - (window - 1), 0)
    key_seg = lax.dynamic_slice_in_dim(segs, first, window, 0)
    key_index = lax.dynamic_slice_in_dim(index, first, window, 0)

    qkv_full, qkv_steps = ring_gather(
        jnp.concatenate([query_weight, key_matrix, value_matrix], axis=1)
    )
    gains = gain_gather(jnp.stack([attn_gain, mlp_gain])).astype(F32)
    gain_one, gain_two = gains[0], gains[1]
    source_all = head_gather(tokens).astype(F32)
    out_full, out_steps = ring_gather(after(out_weight.T, qkv_steps[-2][0]))
    gate_full, gate_steps = ring_gather(after(gate_weight, qkv_steps[-1][0]))
    up_full, up_steps = ring_gather(after(up_weight, gate_steps[1][0]))
    down_full, down_steps = ring_gather(after(down_weight.T, up_steps[1][0]))
    cotangent_all = head_gather(after(cotangent, qkv_steps[-1][0]))

    inverse_all = norm_scale(source_all)
    normed_all = (source_all * inverse_all * gain_one).astype(BF)
    source = source_all[:own_rows]
    inverse_one = inverse_all[:own_rows]
    linear = simple_product(normed_all, qkv_full)
    table = rotary_table(own_pos, width)
    queries = apply_rotary(
        linear[:, :query_cols].reshape(rows, repeats, width), table, 1.0
    ).astype(BF)
    key_rot = apply_rotary(
        linear[:, query_cols : query_cols + width].reshape(rows, 1, width), table, 1.0
    ).reshape(rows, width)
    pair = jnp.concatenate(
        [key_rot.astype(BF), linear[:, query_cols + width :].astype(BF)], axis=1
    )
    pairs_all, _ = ring_gather(pair)
    pairs = lax.dynamic_slice_in_dim(pairs_all, first * rows, window * rows, 0)
    masks = [
        (own_seg[:, None] == key_seg[j][None, :]) & (key_index[j][None, :] <= own_index[:, None])
        for j in range(window)
    ]
    key_parts = [pairs[j * rows : (j + 1) * rows, :width] for j in range(window)]
    value_parts = [pairs[j * rows : (j + 1) * rows, width:] for j in range(window)]
    run_max = jnp.full((repeats, rows), MASKED, F32)
    run_total = jnp.zeros((repeats, rows), F32)
    for j in range(window):
        scores = block_scores(queries, key_parts[j], masks[j])
        new_max = jnp.maximum(run_max, jnp.max(scores, axis=-1))
        run_total = run_total * jnp.exp(run_max - new_max) + jnp.sum(
            jnp.where(masks[j][None], jnp.exp(scores - new_max[..., None]), 0.0), axis=-1
        )
        run_max = new_max
    log_total = run_max + jnp.log(run_total)
    attn_full = jnp.zeros((rows, repeats, width), F32)
    for j in range(window):
        scores = block_scores(queries, key_parts[j], masks[j])
        probs = jnp.exp(scores - log_total[..., None]).astype(BF)
        attn_full = attn_full + jnp.einsum(
            "rqk,kd->qrd", probs, value_parts[j], preferred_element_type=F32
        )
    attn_low = attn_full.reshape(rows, query_cols).astype(BF)
    residual = source + head_sum(times_rows(attn_low, out_full))

    inverse_two = norm_scale(residual)
    normed_two = (residual * inverse_two * gain_two).astype(BF)
    normed_two_all = head_gather(normed_two)
    gate_lin = simple_product(normed_two_all, gate_full)
    up_lin = simple_product(normed_two_all, up_full)
    sigmoid_gate = jax.nn.sigmoid(gate_lin)
    silu_gate = gate_lin * sigmoid_gate
    hidden = (silu_gate * up_lin).astype(BF)
    down_grad = ring_sum(outer_sum(cotangent_all, hidden).astype(BF)).T
    hidden_grad = simple_product(cotangent_all, down_full)
    gate_act_grad = (
        hidden_grad * up_lin * sigmoid_gate * (1.0 + gate_lin * (1.0 - sigmoid_gate))
    ).astype(BF)
    up_act_grad = (hidden_grad * silu_gate).astype(BF)
    normed_two_grad = head_sum(
        times_rows(gate_act_grad, gate_full) + times_rows(up_act_grad, up_full)
    )
    gate_grad = ring_sum(outer_sum(normed_two_all, gate_act_grad).astype(BF))
    up_grad = ring_sum(outer_sum(normed_two_all, up_act_grad).astype(BF))
    layer_out = (residual + head_sum(times_rows(hidden, down_full))).astype(BF)

    residual_grad = cotangent.astype(F32) + norm_back(
        residual, gain_two, inverse_two, normed_two_grad
    )
    mlp_gain_grad = gain_sum(jnp.sum(normed_two_grad * residual * inverse_two, axis=0))
    branch_all = head_gather(residual_grad.astype(BF))
    out_grad = ring_sum(outer_sum(branch_all, attn_low).astype(BF)).T

    attn_grad = simple_product(branch_all, out_full).astype(BF).reshape(rows, repeats, width)
    row_delta = jnp.einsum("qrd,qrd->rq", attn_grad.astype(F32), attn_full)
    score_scale = 1.0 / math.sqrt(width)
    query_rot_grad = jnp.zeros((rows, repeats, width), F32)
    pair_grads = []
    for j in range(window):
        scores = block_scores(queries, key_parts[j], masks[j])
        probs = jnp.exp(scores - log_total[..., None])
        prob_grad = jnp.einsum("qrd,kd->rqk", attn_grad, value_parts[j], preferred_element_type=F32)
        score_grad = (probs * (prob_grad - row_delta[..., None])).astype(BF)
        query_rot_grad = (
            query_rot_grad
            + jnp.einsum("rqk,kd->qrd", score_grad, key_parts[j], preferred_element_type=F32)
            * score_scale
        )
        key_grad = (
            jnp.einsum("rqk,qrd->kd", score_grad, queries, preferred_element_type=F32) * score_scale
        )
        value_grad = jnp.einsum(
            "rqk,qrd->kd", probs.astype(BF), attn_grad, preferred_element_type=F32
        )
        pair_grads.append(jnp.concatenate([key_grad, value_grad], axis=1).astype(BF))
    pair_grad = jnp.zeros((blocks * rows, 2 * width), BF)
    pair_grad = lax.dynamic_update_slice_in_dim(
        pair_grad, jnp.concatenate(pair_grads, axis=0), first * rows, 0
    )
    pair_grad = ring_sum(pair_grad)
    query_lin_grad = apply_rotary(query_rot_grad, table, -1.0).astype(BF).reshape(rows, query_cols)
    key_lin_grad = apply_rotary(pair_grad[:, :width].reshape(rows, 1, width), table, -1.0)
    pair_lin_grad = jnp.concatenate(
        [key_lin_grad.reshape(rows, width), pair_grad[:, width:]], axis=1
    ).astype(BF)
    query_grad = ring_sum(outer_sum(normed_all, query_lin_grad).astype(BF))
    pair_weight_grad = ring_sum(outer_sum(normed_all, pair_lin_grad).astype(BF))
    normed_grad_part = times_rows(query_lin_grad, qkv_full[:, :query_cols]) + times_rows(
        pair_lin_grad, qkv_full[:, query_cols:]
    )
    attn_gain_grad = gain_sum(jnp.sum(normed_grad_part * source_all * inverse_all, axis=0))
    normed_grad = head_sum(normed_grad_part)
    tokens_grad = residual_grad + norm_back(source, gain_one, inverse_one, normed_grad)
    return (
        layer_out,
        tokens_grad,
        attn_gain_grad,
        query_grad,
        pair_weight_grad[:, :width],
        pair_weight_grad[:, width:],
        out_grad,
        mlp_gain_grad,
        gate_grad,
        up_grad,
        down_grad,
    )


def solution(mesh):
    return jax.shard_map(
        local,
        mesh=mesh,
        in_specs=(
            P(("blk", "head"), None),
            P("blk"),
            P("blk", "head"),
            P("blk", "head"),
            P("blk", "head"),
            P("head", "blk"),
            P("blk"),
            P("blk", "head"),
            P("blk", "head"),
            P("head", "blk"),
            P(),
            P(),
            P(("blk", "head"), None),
        ),
        out_specs=(
            P(("blk", "head"), None),
            P(("blk", "head"), None),
            P("blk"),
            P("blk", "head"),
            P("blk", "head"),
            P("blk", "head"),
            P("head", "blk"),
            P("blk"),
            P("blk", "head"),
            P("blk", "head"),
            P("head", "blk"),
        ),
        check_vma=False,
    )
```

```python
import math

import jax
import jax.numpy as jnp
from jax import lax
from jax.experimental import pallas as pl
from jax.experimental.pallas import tpu as pltpu
from jax.sharding import PartitionSpec as P

QUERY_HEADS_ALL = 8
KEY_VALUE_HEADS = 4
HEAD_WIDTH = 256
SEQ = 4096

EPSILON = 1e-06
THETA_BASE = 1000042.0
MASKED = -1e30
BF = jnp.bfloat16
F32 = jnp.float32


def after(value, *deps):
    return lax.optimization_barrier((value, *deps))[0]


def cycle_order(count):
    return list(range(0, count, 2)) + list(range(count - 1, 0, -2))


def cycle_place(index, count):
    return jnp.where(index % 2 == 0, index // 2, count // 2 + (count - 1 - index) // 2)


def cycle_owner(place, count):
    place = lax.rem(place + 2 * count, count)
    return jnp.where(place < count // 2, 2 * place, 2 * (count - 1 - place) + 1)


def ring_routes(count):
    order = cycle_order(count)
    up = [(order[i], order[(i + 1) % count]) for i in range(count)]
    return up, [(b, a) for a, b in up]


def ring_gather(shard):
    count = lax.axis_size("blk")
    me = lax.axis_index("blk")
    place = cycle_place(me, count)
    up, down = ring_routes(count)
    rows = shard.shape[0]
    half = rows // 2
    out = jnp.zeros((count * rows, *shard.shape[1:]), shard.dtype)
    out = lax.dynamic_update_slice_in_dim(out, shard, me * rows, 0)
    left, right = shard, shard
    steps = []
    for step in range(1, count // 2 + 1):
        if step < count // 2:
            left = lax.ppermute(left, "blk", up)
            right = lax.ppermute(right, "blk", down)
            low, high = cycle_owner(place - step, count), cycle_owner(place + step, count)
            out = lax.dynamic_update_slice_in_dim(out, left, low * rows, 0)
            out = lax.dynamic_update_slice_in_dim(out, right, high * rows, 0)
        else:
            left = lax.ppermute(left[:half], "blk", up)
            right = lax.ppermute(right[half:], "blk", down)
            far = cycle_owner(place - step, count)
            out = lax.dynamic_update_slice_in_dim(out, left, far * rows, 0)
            out = lax.dynamic_update_slice_in_dim(out, right, far * rows + half, 0)
        steps.append((left, right))
    return out, steps


def ring_sum(blocks):
    count = lax.axis_size("blk")
    me = lax.axis_index("blk")
    place = cycle_place(me, count)
    up, down = ring_routes(count)
    rows = blocks.shape[0] // count
    half = rows // 2

    def part(offset):
        return lax.dynamic_slice_in_dim(
            blocks, cycle_owner(place + offset, count) * rows, rows, 0
        )

    far = part(count // 2)
    left = lax.ppermute(far[:half], "blk", up)
    right = lax.ppermute(far[half:], "blk", down)
    for step in range(count // 2 - 1, -1, -1):
        if step == count // 2 - 1:
            low, high = part(step), part(-step)
            left = jnp.concatenate([(low[:half].astype(F32) + left.astype(F32)).astype(BF), low[half:]])
            right = jnp.concatenate([high[:half], (high[half:].astype(F32) + right.astype(F32)).astype(BF)])
        elif step > 0:
            left = (part(step).astype(F32) + left.astype(F32)).astype(BF)
            right = (part(-step).astype(F32) + right.astype(F32)).astype(BF)
        else:
            return part(0).astype(F32) + left.astype(F32) + right.astype(F32)
        left = lax.ppermute(left, "blk", up)
        right = lax.ppermute(right, "blk", down)


def flip(value, axis, bit):
    return lax.ppermute(value, axis, [(i, i ^ bit) for i in range(lax.axis_size(axis))])


def head_gather(rows):
    other = flip(rows, "head", 2)
    pair = jnp.concatenate([rows, other], axis=0)
    beside = flip(pair, "head", 1)
    count = rows.shape[0]
    return jnp.concatenate([rows, beside[:count], other, beside[count:]], axis=0)


def head_sum(partial):
    low = partial.astype(BF).reshape(2, 2, partial.shape[0] // 4, *partial.shape[1:])
    near = flip(low[:, 1], "head", 1)
    pair = low[:, 0].astype(F32) + near.astype(F32)
    far = flip(pair[1].astype(BF), "head", 2)
    return pair[0] + far.astype(F32)


def slots(values, head_index):
    values = values.reshape(values.shape[0], 2, 2, values.shape[-1])
    values = jnp.where(head_index % 2 == 1, values[:, :, ::-1], values)
    values = jnp.where(head_index // 2 == 1, values[:, ::-1], values)
    return values.reshape(values.shape[0], -1)


def gain_gather(gains):
    count = lax.axis_size("blk")
    me = lax.axis_index("blk")
    bit = 1
    while bit < count:
        other = flip(gains, "blk", bit)
        low = jnp.concatenate([gains, other], axis=1)
        high = jnp.concatenate([other, gains], axis=1)
        gains = jnp.where((me // bit) % 2 == 0, low, high)
        bit *= 2
    return gains


def gain_sum(grad):
    for bit in (1, 2):
        grad = grad + flip(grad, "head", bit)
    count = lax.axis_size("blk")
    me = lax.axis_index("blk")
    bit = count // 2
    while bit:
        size = grad.shape[0] // 2
        upper = (me // bit) % 2 == 1
        keep = jnp.where(upper, grad[size:], grad[:size])
        send = jnp.where(upper, grad[:size], grad[size:])
        grad = keep + flip(send, "blk", bit)
        bit //= 2
    return grad


def rotary_table(token_pos, width):
    half_size = width // 2
    frequency = THETA_BASE ** (-2.0 * jnp.arange(half_size, dtype=F32) / width)
    angles = token_pos.astype(F32)[:, None] * frequency[None, :]
    return jnp.cos(angles)[:, None, :], jnp.sin(angles)[:, None, :]


def apply_rotary(values, table, direction):
    cosine, sine_part = table
    sine_part = sine_part * direction
    half_size = values.shape[-1] // 2
    first_half = values[..., :half_size]
    second_half = values[..., half_size:]
    return jnp.concatenate(
        [
            first_half * cosine - second_half * sine_part,
            second_half * cosine + first_half * sine_part,
        ],
        axis=-1,
    )


def norm_scale(values):
    return lax.rsqrt(jnp.mean(values * values, axis=-1, keepdims=True) + EPSILON)


def norm_back(values, gain_vec, inverse, upstream):
    weighted = upstream * gain_vec
    inner_mean = jnp.mean(weighted * values, axis=-1, keepdims=True)
    return inverse * weighted - values * (inverse * inverse * inverse) * inner_mean


def simple_product(matrix_a, matrix_b):
    return jnp.dot(matrix_a, matrix_b, preferred_element_type=F32)


def outer_sum(matrix_a, matrix_b):
    return lax.dot_general(
        matrix_a, matrix_b, (((0,), (0,)), ((), ())), preferred_element_type=F32
    )


def times_rows(matrix_a, matrix_b):
    return lax.dot_general(
        matrix_a, matrix_b, (((1,), (1,)), ((), ())), preferred_element_type=F32
    )


CHUNK = 256


def contract(a, b, dim_a, dim_b):
    return lax.dot_general(
        a, b, (((dim_a,), (dim_b,)), ((), ())), preferred_element_type=F32
    )


def attend_kernel(repeats, width, kind, q_ref, kv_ref, low_ref, high_ref, index_ref, out_ref, lse_ref, acc, top, total):
    step = pl.program_id(0)
    rows = q_ref.shape[0]

    @pl.when(step == 0)
    def _():
        acc[...] = jnp.zeros_like(acc)
        top[...] = jnp.full_like(top, MASKED)
        total[...] = jnp.zeros_like(total)

    def block(masked):
        keys = kv_ref[:, :width]
        values = kv_ref[:, width:]
        for start in range(0, rows, CHUNK):
            part = pl.ds(start, CHUNK)
            if masked:
                index = index_ref[0]
                allowed = (index >= low_ref[part, :]) & (index <= high_ref[part, :])
            for r in range(repeats):
                cols = slice(r * width, (r + 1) * width)
                scores = contract(q_ref[part, cols], keys, 1, 1)
                if masked:
                    scores = jnp.where(allowed, scores, MASKED)
                old = top[r, part, :]
                new = jnp.maximum(old, jnp.max(scores, axis=1, keepdims=True))
                probs = jnp.exp(scores - new)
                if masked:
                    probs = jnp.where(allowed, probs, 0.0)
                factor = jnp.exp(old - new)
                total[r, part, :] = total[r, part, :] * factor + jnp.sum(probs, axis=1, keepdims=True)
                top[r, part, :] = new
                acc[part, cols] = acc[part, cols] * factor + contract(probs.astype(BF), values, 1, 0)

    pl.when(kind[step] == 1)(lambda: block(False))
    pl.when(kind[step] == 2)(lambda: block(True))

    @pl.when(step == pl.num_programs(0) - 1)
    def _():
        for r in range(repeats):
            cols = slice(r * width, (r + 1) * width)
            out_ref[:, cols] = acc[:, cols] / total[r]
            lse_ref[r] = top[r] + jnp.log(total[r])


def attend(kind, queries, pairs, low, high, index, repeats, width):
    rows = queries.shape[0]
    blocks = pairs.shape[0] // rows
    whole = lambda shape: pl.BlockSpec(shape, lambda j, kind: (0,) * len(shape))
    return pl.pallas_call(
        lambda *refs: attend_kernel(repeats, width, *refs),
        grid_spec=pltpu.PrefetchScalarGridSpec(
            num_scalar_prefetch=1,
            grid=(blocks,),
            in_specs=[
                whole((rows, repeats * width)),
                pl.BlockSpec((rows, 2 * width), lambda j, kind: (j, 0)),
                whole((rows, 1)),
                whole((rows, 1)),
                pl.BlockSpec((1, 1, rows), lambda j, kind: (j, 0, 0)),
            ],
            out_specs=[whole((rows, repeats * width)), whole((repeats, rows, 1))],
            scratch_shapes=[
                pltpu.VMEM((rows, repeats * width), F32),
                pltpu.VMEM((repeats, rows, 1), F32),
                pltpu.VMEM((repeats, rows, 1), F32),
            ],
        ),
        out_shape=[
            jax.ShapeDtypeStruct((rows, repeats * width), F32),
            jax.ShapeDtypeStruct((repeats, rows, 1), F32),
        ],
        compiler_params=pltpu.CompilerParams(vmem_limit_bytes=40 * 2**20),
        cost_estimate=pl.CostEstimate(
            flops=4 * repeats * width * rows * rows * 7,
            bytes_accessed=12 * 2**20,
            transcendentals=repeats * rows * rows * 7,
        ),
        name="attend",
    )(kind, queries, pairs, low, high, index)


def attend_back_kernel(
    repeats, width, kind, q_ref, kv_ref, up_ref, low_ref, high_ref, index_ref, lse_ref, delta_ref, dq_ref, dkv_ref
):
    step = pl.program_id(0)
    rows = q_ref.shape[0]

    @pl.when(step == 0)
    def _():
        dq_ref[...] = jnp.zeros_like(dq_ref)

    def block(masked):
        for start in range(0, rows, CHUNK):
            part = pl.ds(start, CHUNK)
            keys = kv_ref[part, :width]
            values = kv_ref[part, width:]
            key_grad = jnp.zeros((CHUNK, width), F32)
            value_grad = jnp.zeros((CHUNK, width), F32)
            if masked:
                index = index_ref[0, part, :]
                allowed = (index >= low_ref[...]) & (index <= high_ref[...])
            for r in range(repeats):
                cols = slice(r * width, (r + 1) * width)
                queries, upstream = q_ref[:, cols], up_ref[:, cols]
                probs = jnp.exp(contract(keys, queries, 1, 1) - lse_ref[r])
                if masked:
                    probs = jnp.where(allowed, probs, 0.0)
                prob_grad = contract(values, upstream, 1, 1)
                score_grad = (probs * (prob_grad - delta_ref[r])).astype(BF)
                value_grad += contract(probs.astype(BF), upstream, 1, 0)
                key_grad += contract(score_grad, queries, 1, 0)
                dq_ref[:, cols] += contract(score_grad, keys, 0, 0)
            dkv_ref[part, :width] = key_grad.astype(BF)
            dkv_ref[part, width:] = value_grad.astype(BF)

    @pl.when(kind[step] == 0)
    def _():
        dkv_ref[...] = jnp.zeros_like(dkv_ref)

    pl.when(kind[step] == 1)(lambda: block(False))
    pl.when(kind[step] == 2)(lambda: block(True))


def attend_back(kind, queries, pairs, upstream, low, high, index, lse, delta, repeats, width):
    rows = queries.shape[0]
    blocks = pairs.shape[0] // rows
    whole = lambda shape: pl.BlockSpec(shape, lambda j, kind: (0,) * len(shape))
    return pl.pallas_call(
        lambda *refs: attend_back_kernel(repeats, width, *refs),
        grid_spec=pltpu.PrefetchScalarGridSpec(
            num_scalar_prefetch=1,
            grid=(blocks,),
            in_specs=[
                whole((rows, repeats * width)),
                pl.BlockSpec((rows, 2 * width), lambda j, kind: (j, 0)),
                whole((rows, repeats * width)),
                whole((1, rows)),
                whole((1, rows)),
                pl.BlockSpec((1, rows, 1), lambda j, kind: (j, 0, 0)),
                whole((repeats, 1, rows)),
                whole((repeats, 1, rows)),
            ],
            out_specs=[
                whole((rows, repeats * width)),
                pl.BlockSpec((rows, 2 * width), lambda j, kind: (j, 0)),
            ],
        ),
        out_shape=[
            jax.ShapeDtypeStruct((rows, repeats * width), F32),
            jax.ShapeDtypeStruct((blocks * rows, 2 * width), BF),
        ],
        compiler_params=pltpu.CompilerParams(vmem_limit_bytes=40 * 2**20),
        cost_estimate=pl.CostEstimate(
            flops=10 * repeats * width * rows * rows * 7,
            bytes_accessed=20 * 2**20,
            transcendentals=repeats * rows * rows * 7,
        ),
        name="attend_back",
    )(kind, queries, pairs, upstream, low, high, index, lse, delta)


def local(
    tokens,
    attn_gain,
    query_weight,
    key_matrix,
    value_matrix,
    out_weight,
    mlp_gain,
    gate_weight,
    up_weight,
    down_weight,
    segment_ids,
    positions,
    cotangent,
):
    heads = lax.axis_size("head")
    blocks = lax.axis_size("blk")
    blk = lax.axis_index("blk")
    head = lax.axis_index("head")
    own_rows = tokens.shape[0]
    rows = own_rows * heads
    width = HEAD_WIDTH
    repeats = QUERY_HEADS_ALL // KEY_VALUE_HEADS
    query_cols = query_weight.shape[1]

    segs = slots(segment_ids.reshape(blocks, heads, own_rows), head)
    poss = slots(positions.reshape(blocks, heads, own_rows), head)
    index = slots(jnp.arange(blocks * rows, dtype=jnp.int32).reshape(blocks, heads, own_rows), head)
    own_seg = lax.dynamic_index_in_dim(segs, blk, 0, False)
    own_pos = lax.dynamic_index_in_dim(poss, blk, 0, False)
    high = lax.dynamic_index_in_dim(index, blk, 0, False)
    low = jnp.sum(
        (segment_ids[None, :] < own_seg[:, None]).astype(jnp.int32), axis=1
    )
    block_seg = segment_ids.reshape(blocks, rows)
    seg_first, seg_last = block_seg[:, 0], block_seg[:, -1]
    ids = jnp.arange(blocks, dtype=jnp.int32)
    some = (ids <= blk) & (seg_last >= seg_first[blk])
    every = (ids < blk) & (seg_first == seg_last[blk])
    kind = jnp.where(every, 1, jnp.where(some, 2, 0)).astype(jnp.int32)
    table = rotary_table(own_pos, width)

    qkv_full, qkv_steps = ring_gather(
        jnp.concatenate([query_weight, key_matrix, value_matrix], axis=1)
    )
    gains = gain_gather(jnp.stack([attn_gain, mlp_gain])).astype(F32)
    gain_one, gain_two = gains[0], gains[1]
    source_all = head_gather(tokens).astype(F32)
    out_full, out_steps = ring_gather(after(out_weight.T, qkv_steps[-2][0]))
    gate_full, gate_steps = ring_gather(after(gate_weight, qkv_steps[-1][0]))
    up_full, up_steps = ring_gather(after(up_weight, gate_steps[1][0]))
    down_full, down_steps = ring_gather(after(down_weight.T, up_steps[1][0]))
    cotangent_all = head_gather(after(cotangent, qkv_steps[-1][0]))

    inverse_all = norm_scale(source_all)
    normed_all = (source_all * inverse_all * gain_one).astype(BF)
    source = source_all[:own_rows]
    inverse_one = inverse_all[:own_rows]
    linear = simple_product(normed_all, qkv_full)
    score_scale = 1.0 / math.sqrt(width)
    queries = (
        apply_rotary(linear[:, :query_cols].reshape(rows, repeats, width), table, 1.0).astype(BF)
        * score_scale
    ).reshape(rows, query_cols)
    key_rot = apply_rotary(
        linear[:, query_cols : query_cols + width].reshape(rows, 1, width), table, 1.0
    ).reshape(rows, width)
    pair = jnp.concatenate(
        [key_rot.astype(BF), linear[:, query_cols + width :].astype(BF)], axis=1
    )
    pairs, _ = ring_gather(pair)
    index = index.reshape(blocks, 1, rows)
    attn_full, lse = attend(kind, queries, pairs, low[:, None], high[:, None], index, repeats, width)
    attn_low = attn_full.astype(BF)
    residual = source + head_sum(times_rows(attn_low, out_full))

    inverse_two = norm_scale(residual)
    normed_two = (residual * inverse_two * gain_two).astype(BF)
    normed_two_all = head_gather(normed_two)
    gate_lin = simple_product(normed_two_all, gate_full)
    up_lin = simple_product(normed_two_all, up_full)
    sigmoid_gate = jax.nn.sigmoid(gate_lin)
    silu_gate = gate_lin * sigmoid_gate
    hidden = (silu_gate * up_lin).astype(BF)
    down_grad = ring_sum(outer_sum(cotangent_all, hidden).astype(BF)).T
    hidden_grad = simple_product(cotangent_all, down_full)
    gate_act_grad = (
        hidden_grad * up_lin * sigmoid_gate * (1.0 + gate_lin * (1.0 - sigmoid_gate))
    ).astype(BF)
    up_act_grad = (hidden_grad * silu_gate).astype(BF)
    normed_two_grad = head_sum(
        times_rows(gate_act_grad, gate_full) + times_rows(up_act_grad, up_full)
    )
    gate_grad = ring_sum(outer_sum(normed_two_all, gate_act_grad).astype(BF))
    up_grad = ring_sum(outer_sum(normed_two_all, up_act_grad).astype(BF))
    layer_out = (residual + head_sum(times_rows(hidden, down_full))).astype(BF)

    residual_grad = cotangent.astype(F32) + norm_back(
        residual, gain_two, inverse_two, normed_two_grad
    )
    mlp_gain_grad = gain_sum(jnp.sum(normed_two_grad * residual * inverse_two, axis=0))
    branch_all = head_gather(residual_grad.astype(BF))
    out_grad = ring_sum(outer_sum(branch_all, attn_low).astype(BF)).T

    attn_grad = simple_product(branch_all, out_full).astype(BF)
    row_delta = jnp.sum(
        (attn_grad.astype(F32) * attn_full).reshape(rows, repeats, width), axis=-1
    ).T.reshape(repeats, 1, rows)
    query_rot_grad, pair_grad = attend_back(
        kind,
        queries,
        pairs,
        attn_grad,
        low[None, :],
        high[None, :],
        index.reshape(blocks, rows, 1),
        lse.reshape(repeats, 1, rows),
        row_delta,
        repeats,
        width,
    )
    pair_grad = ring_sum(pair_grad)
    query_lin_grad = (
        apply_rotary(query_rot_grad.reshape(rows, repeats, width) * score_scale, table, -1.0)
        .astype(BF)
        .reshape(rows, query_cols)
    )
    key_lin_grad = apply_rotary(pair_grad[:, :width].reshape(rows, 1, width), table, -1.0)
    pair_lin_grad = jnp.concatenate(
        [key_lin_grad.reshape(rows, width), pair_grad[:, width:]], axis=1
    ).astype(BF)
    query_grad = ring_sum(outer_sum(normed_all, query_lin_grad).astype(BF))
    pair_weight_grad = ring_sum(outer_sum(normed_all, pair_lin_grad).astype(BF))
    normed_grad_part = times_rows(query_lin_grad, qkv_full[:, :query_cols]) + times_rows(
        pair_lin_grad, qkv_full[:, query_cols:]
    )
    attn_gain_grad = gain_sum(jnp.sum(normed_grad_part * source_all * inverse_all, axis=0))
    normed_grad = head_sum(normed_grad_part)
    tokens_grad = residual_grad + norm_back(source, gain_one, inverse_one, normed_grad)
    return (
        layer_out,
        tokens_grad,
        attn_gain_grad,
        query_grad,
        pair_weight_grad[:, :width],
        pair_weight_grad[:, width:],
        out_grad,
        mlp_gain_grad,
        gate_grad,
        up_grad,
        down_grad,
    )


def solution(mesh):
    return jax.shard_map(
        local,
        mesh=mesh,
        in_specs=(
            P(("blk", "head"), None),
            P("blk"),
            P("blk", "head"),
            P("blk", "head"),
            P("blk", "head"),
            P("head", "blk"),
            P("blk"),
            P("blk", "head"),
            P("blk", "head"),
            P("head", "blk"),
            P(),
            P(),
            P(("blk", "head"), None),
        ),
        out_specs=(
            P(("blk", "head"), None),
            P(("blk", "head"), None),
            P("blk"),
            P("blk", "head"),
            P("blk", "head"),
            P("blk", "head"),
            P("head", "blk"),
            P("blk"),
            P("blk", "head"),
            P("blk", "head"),
            P("head", "blk"),
        ),
        check_vma=False,
    )
```

```python
import math

import jax
import jax.numpy as jnp
from jax import lax
from jax.experimental import pallas as pl
from jax.experimental.pallas import tpu as pltpu
from jax.sharding import PartitionSpec as P

QUERY_HEADS_ALL = 8
KEY_VALUE_HEADS = 4
HEAD_WIDTH = 256
SEQ = 4096

EPSILON = 1e-06
THETA_BASE = 1000042.0
MASKED = -1e30
PAIR_BIT = 1
BF = jnp.bfloat16
F32 = jnp.float32


def after(value, *deps):
    return lax.optimization_barrier((value, *deps))[0]


def cycle_order(count):
    return list(range(0, count, 2)) + list(range(count - 1, 0, -2))


def cycle_place(index, count):
    return jnp.where(index % 2 == 0, index // 2, count // 2 + (count - 1 - index) // 2)


def cycle_owner(place, count):
    place = lax.rem(place + 2 * count, count)
    return jnp.where(place < count // 2, 2 * place, 2 * (count - 1 - place) + 1)


def ring_routes(count):
    order = cycle_order(count)
    up = [(order[i], order[(i + 1) % count]) for i in range(count)]
    return up, [(b, a) for a, b in up]


def barrier(*values):
    return lax.optimization_barrier(values)


def join(movers, *values):
    flights = [mover.flight() for mover in movers]
    flat = [value for flight in flights for value in flight]
    done = lax.optimization_barrier((*flat, *values))
    place = 0
    for mover, flight in zip(movers, flights):
        mover.land(list(done[place : place + len(flight)]))
        place += len(flight)
    rest = done[place:]
    return rest[0] if len(rest) == 1 else rest


class RingGather:
    def __init__(self, shard):
        self.count = lax.axis_size("blk")
        self.me = lax.axis_index("blk")
        self.place = cycle_place(self.me, self.count)
        self.routes = ring_routes(self.count)
        self.shard = self.left = self.right = shard
        self.step = 0
        self.parts = []

    def go(self):
        self.step += 1
        half = self.shard.shape[0] // 2
        left, right = self.left, self.right
        if self.step == self.count // 2:
            left, right = left[:half], right[half:]
        self.left = lax.ppermute(left, "blk", self.routes[0])
        self.right = lax.ppermute(right, "blk", self.routes[1])

    def rest(self):
        while self.step < self.count // 2 - 1:
            self.go()
            join([self])

    def flight(self):
        return [self.left, self.right]

    def land(self, values):
        self.left, self.right = values
        self.parts.append((self.step, self.left, self.right))

    def full(self):
        rows = self.shard.shape[0]
        out = jnp.zeros((self.count * rows, *self.shard.shape[1:]), self.shard.dtype)
        out = lax.dynamic_update_slice_in_dim(out, self.shard, self.me * rows, 0)
        for step, left, right in self.parts:
            low = cycle_owner(self.place - step, self.count) * rows
            high = cycle_owner(self.place + step, self.count) * rows
            if step == self.count // 2:
                high = low + rows // 2
            out = lax.dynamic_update_slice_in_dim(out, left, low, 0)
            out = lax.dynamic_update_slice_in_dim(out, right, high, 0)
        return out


class RingSum:
    def __init__(self, blocks):
        self.count = lax.axis_size("blk")
        self.place = cycle_place(lax.axis_index("blk"), self.count)
        self.routes = ring_routes(self.count)
        self.blocks = blocks
        self.rows = blocks.shape[0] // self.count
        self.step = self.count // 2

    def part(self, offset):
        return lax.dynamic_slice_in_dim(
            self.blocks, cycle_owner(self.place + offset, self.count) * self.rows, self.rows, 0
        )

    def go(self):
        half = self.rows // 2
        if self.step == self.count // 2:
            far = self.part(self.step)
            left, right = far[:half], far[half:]
        else:
            low, high = self.part(self.step), self.part(-self.step)
            left, right = self.left.astype(F32), self.right.astype(F32)
            if self.step == self.count // 2 - 1:
                left = jnp.concatenate([(low[:half].astype(F32) + left).astype(BF), low[half:]])
                right = jnp.concatenate([high[:half], (high[half:].astype(F32) + right).astype(BF)])
            else:
                left = (low.astype(F32) + left).astype(BF)
                right = (high.astype(F32) + right).astype(BF)
        self.left = lax.ppermute(left, "blk", self.routes[0])
        self.right = lax.ppermute(right, "blk", self.routes[1])
        self.step -= 1
        return left, right

    def rest(self):
        while self.step > 1:
            self.go()
            join([self])

    def flight(self):
        return [self.left, self.right]

    def land(self, values):
        self.left, self.right = values

    def total(self):
        return self.part(0).astype(F32) + self.left.astype(F32) + self.right.astype(F32)


def flip(value, axis, bit):
    return lax.ppermute(value, axis, [(i, i ^ bit) for i in range(lax.axis_size(axis))])


def head_rest(rows, other):
    pair = jnp.concatenate([rows, other], axis=0)
    return rows, other, flip(pair, "head", 1)


def head_all(rows, other, beside):
    count = rows.shape[0]
    return jnp.concatenate([rows, beside[:count], other, beside[count:]], axis=0)


def head_near(partial):
    low = partial.astype(BF).reshape(2, 2, partial.shape[0] // 4, *partial.shape[1:])
    return low[:, 0], flip(low[:, 1], "head", 1)


def head_far(kept, near):
    pair = kept.astype(F32) + near.astype(F32)
    return pair[0], flip(pair[1].astype(BF), "head", 2)


def slots(values, head_index):
    values = values.reshape(values.shape[0], 2, 2, values.shape[-1])
    values = jnp.where(head_index % 2 == 1, values[:, :, ::-1], values)
    values = jnp.where(head_index // 2 == 1, values[:, ::-1], values)
    return values.reshape(values.shape[0], -1)


def gain_hop(gains, bit):
    if bit >= lax.axis_size("blk"):
        return gains
    me = lax.axis_index("blk")
    other = flip(gains, "blk", bit)
    low = jnp.concatenate([gains, other], axis=1)
    high = jnp.concatenate([other, gains], axis=1)
    return jnp.where((me // bit) % 2 == 0, low, high)


def gain_back(grads, bit):
    low, high = jnp.split(grads, 2, axis=1)
    upper = (lax.axis_index("blk") // bit) % 2 == 1
    return jnp.where(upper, high, low) + flip(jnp.where(upper, low, high), "blk", bit)


def rotary_table(token_pos, width):
    half_size = width // 2
    frequency = THETA_BASE ** (-2.0 * jnp.arange(half_size, dtype=F32) / width)
    angles = token_pos.astype(F32)[:, None] * frequency[None, :]
    return jnp.cos(angles), jnp.sin(angles)


def apply_rotary(values, table, direction):
    cosine, sine_part = table
    sine_part = sine_part * direction
    half = cosine.shape[1]
    out = []
    for start in range(0, values.shape[1], 2 * half):
        first = values[:, start : start + half]
        second = values[:, start + half : start + 2 * half]
        out += [first * cosine - second * sine_part, second * cosine + first * sine_part]
    return jnp.concatenate(out, axis=1)


def norm_scale(values):
    return lax.rsqrt(jnp.mean(values * values, axis=-1, keepdims=True) + EPSILON)


def norm_back(values, gain_vec, inverse, upstream):
    weighted = upstream * gain_vec
    inner_mean = jnp.mean(weighted * values, axis=-1, keepdims=True)
    return inverse * weighted - values * (inverse * inverse * inverse) * inner_mean


def simple_product(matrix_a, matrix_b):
    return jnp.dot(matrix_a, matrix_b, preferred_element_type=F32)


def outer_sum(matrix_a, matrix_b):
    return lax.dot_general(
        matrix_a, matrix_b, (((0,), (0,)), ((), ())), preferred_element_type=F32
    )


def times_rows(matrix_a, matrix_b):
    return lax.dot_general(
        matrix_a, matrix_b, (((1,), (1,)), ((), ())), preferred_element_type=F32
    )


def pair_side(blk):
    return jnp.where((blk & PAIR_BIT) != 0, 1, 0)


def halves(shard, axis):
    side = pair_side(lax.axis_index("blk"))
    low, high = jnp.split(shard, 2, axis=axis)
    return jnp.where(side == 0, low, high), jnp.where(side == 0, high, low)


def plane_groups():
    count = lax.axis_size("blk")
    return [[i for i in range(count) if i & PAIR_BIT == side] for side in (0, PAIR_BIT)]


def group_gather(rows):
    return lax.all_gather(rows, "blk", axis=0, tiled=True, axis_index_groups=plane_groups())


def group_sum(partial):
    return lax.psum_scatter(
        partial.astype(BF),
        "blk",
        scatter_dimension=0,
        tiled=True,
        axis_index_groups=plane_groups(),
    )


def send_half(both):
    mine, other = halves(both, 0)
    return mine, flip(other, "blk", PAIR_BIT)


def narrow_half(mine, other):
    side = pair_side(lax.axis_index("blk"))
    mine, other = mine.astype(F32), other.astype(F32)
    return jnp.concatenate(
        [jnp.where(side == 0, mine, other), jnp.where(side == 0, other, mine)], axis=1
    )


def place_half(mine, other):
    side = pair_side(lax.axis_index("blk"))
    return jnp.concatenate(
        [jnp.where(side == 0, mine, other), jnp.where(side == 0, other, mine)], axis=0
    )


def wide_near(rows):
    return flip(rows, "head", 2), flip(rows, "blk", PAIR_BIT)


def wide_far(near_y, near_z):
    half = near_y.shape[1] // 2
    return flip(near_z[:, :half], "head", 2), flip(near_y[:, half:], "blk", PAIR_BIT)


def wide_rest(rows, near_y, near_z, far):
    far = jnp.concatenate(far, axis=1)
    trio = jnp.concatenate([rows, near_y, near_z], axis=0)
    return jnp.concatenate([trio, flip(trio, "head", 1), far, flip(far, "head", 1)], axis=0)


class WideSum:
    def __init__(self, partial):
        self.rows = partial.shape[0] // 8
        rows = self.rows
        self.far, self.trio = partial[6 * rows : 7 * rows], partial[: 3 * rows]
        self.moving = [
            flip(partial[7 * rows :], "head", 1),
            flip(partial[3 * rows : 6 * rows], "head", 1),
        ]

    def flight(self):
        return self.moving

    def land(self, values):
        self.moving = values

    def go_far(self):
        far = self.far.astype(F32) + self.moving[0].astype(F32)
        self.trio = self.trio.astype(F32) + self.moving[1].astype(F32)
        half = far.shape[1] // 2
        sent = far[:, :half].astype(BF), far[:, half:].astype(BF)
        self.moving = [flip(sent[0], "head", 2), flip(sent[1], "blk", PAIR_BIT)]
        return sent

    def go_near(self):
        rows, half = self.rows, self.trio.shape[1] // 2
        to_z, to_y = (value.astype(F32) for value in self.moving)
        near_y, near_z = self.trio[rows : 2 * rows], self.trio[2 * rows :]
        near_z = jnp.concatenate([near_z[:, :half] + to_z, near_z[:, half:]], axis=1)
        near_y = jnp.concatenate([near_y[:, :half], near_y[:, half:] + to_y], axis=1)
        sent = near_y.astype(BF), near_z.astype(BF)
        self.moving = [flip(sent[0], "head", 2), flip(sent[1], "blk", PAIR_BIT)]
        return sent

    def total(self):
        return self.trio[: self.rows] + self.moving[0].astype(F32) + self.moving[1].astype(F32)


CHUNK = 256
COST = 40


def contract(a, b, dim_a, dim_b):
    return lax.dot_general(
        a, b, (((dim_a,), (dim_b,)), ((), ())), preferred_element_type=F32
    )


def attend_kernel(repeats, width, kind, q_ref, kv_ref, low_ref, high_ref, index_ref, out_ref, lse_ref, acc, top, total):
    step = pl.program_id(0)
    rows = q_ref.shape[0]

    @pl.when(step == 0)
    def _():
        acc[...] = jnp.zeros_like(acc)
        top[...] = jnp.full_like(top, MASKED)
        total[...] = jnp.zeros_like(total)

    def block(masked):
        keys = kv_ref[:, :width]
        values = kv_ref[:, width:]
        for start in range(0, rows, CHUNK):
            part = pl.ds(start, CHUNK)
            if masked:
                index = index_ref[0]
                allowed = (index >= low_ref[part, :]) & (index <= high_ref[part, :])
            for r in range(repeats):
                cols = slice(r * width, (r + 1) * width)
                scores = contract(q_ref[part, cols], keys, 1, 1)
                if masked:
                    scores = jnp.where(allowed, scores, MASKED)
                old = top[r, part, :]
                new = jnp.maximum(old, jnp.max(scores, axis=1, keepdims=True))
                probs = jnp.exp(scores - new)
                if masked:
                    probs = jnp.where(allowed, probs, 0.0)
                factor = jnp.exp(old - new)
                total[r, part, :] = total[r, part, :] * factor + jnp.sum(probs, axis=1, keepdims=True)
                top[r, part, :] = new
                acc[part, cols] = acc[part, cols] * factor + contract(probs.astype(BF), values, 1, 0)

    pl.when(kind[step] == 1)(lambda: block(False))
    pl.when(kind[step] == 2)(lambda: block(True))

    @pl.when(step == pl.num_programs(0) - 1)
    def _():
        for r in range(repeats):
            cols = slice(r * width, (r + 1) * width)
            out_ref[:, cols] = acc[:, cols] / total[r]
            lse_ref[r] = top[r] + jnp.log(total[r])


def attend(kind, queries, pairs, low, high, index, repeats, width):
    rows = queries.shape[0]
    blocks = pairs.shape[0] // rows
    whole = lambda shape: pl.BlockSpec(shape, lambda j, kind: (0,) * len(shape))
    return pl.pallas_call(
        lambda *refs: attend_kernel(repeats, width, *refs),
        grid_spec=pltpu.PrefetchScalarGridSpec(
            num_scalar_prefetch=1,
            grid=(blocks,),
            in_specs=[
                whole((rows, repeats * width)),
                pl.BlockSpec((rows, 2 * width), lambda j, kind: (j, 0)),
                whole((rows, 1)),
                whole((rows, 1)),
                pl.BlockSpec((1, 1, rows), lambda j, kind: (j, 0, 0)),
            ],
            out_specs=[whole((rows, repeats * width)), whole((repeats, rows, 1))],
            scratch_shapes=[
                pltpu.VMEM((rows, repeats * width), F32),
                pltpu.VMEM((repeats, rows, 1), F32),
                pltpu.VMEM((repeats, rows, 1), F32),
            ],
        ),
        out_shape=[
            jax.ShapeDtypeStruct((rows, repeats * width), F32),
            jax.ShapeDtypeStruct((repeats, rows, 1), F32),
        ],
        compiler_params=pltpu.CompilerParams(vmem_limit_bytes=40 * 2**20),
        cost_estimate=pl.CostEstimate(
            flops=COST * repeats * width * rows * rows,
            bytes_accessed=12 * 2**20,
            transcendentals=0,
        ),
        name="attend",
    )(kind, queries, pairs, low, high, index)


def attend_back_kernel(
    repeats, width, kind, q_ref, kv_ref, up_ref, low_ref, high_ref, index_ref, lse_ref, delta_ref, dq_ref, dkv_ref
):
    step = pl.program_id(0)
    rows = q_ref.shape[0]

    @pl.when(step == 0)
    def _():
        dq_ref[...] = jnp.zeros_like(dq_ref)

    def block(masked):
        for start in range(0, rows, CHUNK):
            part = pl.ds(start, CHUNK)
            keys = kv_ref[part, :width]
            values = kv_ref[part, width:]
            key_grad = jnp.zeros((CHUNK, width), F32)
            value_grad = jnp.zeros((CHUNK, width), F32)
            if masked:
                index = index_ref[0, part, :]
                allowed = (index >= low_ref[...]) & (index <= high_ref[...])
            for r in range(repeats):
                cols = slice(r * width, (r + 1) * width)
                queries, upstream = q_ref[:, cols], up_ref[:, cols]
                probs = jnp.exp(contract(keys, queries, 1, 1) - lse_ref[r])
                if masked:
                    probs = jnp.where(allowed, probs, 0.0)
                prob_grad = contract(values, upstream, 1, 1)
                score_grad = (probs * (prob_grad - delta_ref[r])).astype(BF)
                value_grad += contract(probs.astype(BF), upstream, 1, 0)
                key_grad += contract(score_grad, queries, 1, 0)
                dq_ref[:, cols] += contract(score_grad, keys, 0, 0)
            dkv_ref[part, :width] = key_grad.astype(BF)
            dkv_ref[part, width:] = value_grad.astype(BF)

    @pl.when(kind[step] == 0)
    def _():
        dkv_ref[...] = jnp.zeros_like(dkv_ref)

    pl.when(kind[step] == 1)(lambda: block(False))
    pl.when(kind[step] == 2)(lambda: block(True))


def attend_back(kind, queries, pairs, upstream, low, high, index, lse, delta, repeats, width):
    rows = queries.shape[0]
    blocks = pairs.shape[0] // rows
    whole = lambda shape: pl.BlockSpec(shape, lambda j, kind: (0,) * len(shape))
    return pl.pallas_call(
        lambda *refs: attend_back_kernel(repeats, width, *refs),
        grid_spec=pltpu.PrefetchScalarGridSpec(
            num_scalar_prefetch=1,
            grid=(blocks,),
            in_specs=[
                whole((rows, repeats * width)),
                pl.BlockSpec((rows, 2 * width), lambda j, kind: (j, 0)),
                whole((rows, repeats * width)),
                whole((1, rows)),
                whole((1, rows)),
                pl.BlockSpec((1, rows, 1), lambda j, kind: (j, 0, 0)),
                whole((repeats, 1, rows)),
                whole((repeats, 1, rows)),
            ],
            out_specs=[
                whole((rows, repeats * width)),
                pl.BlockSpec((rows, 2 * width), lambda j, kind: (j, 0)),
            ],
        ),
        out_shape=[
            jax.ShapeDtypeStruct((rows, repeats * width), F32),
            jax.ShapeDtypeStruct((blocks * rows, 2 * width), BF),
        ],
        compiler_params=pltpu.CompilerParams(vmem_limit_bytes=40 * 2**20),
        cost_estimate=pl.CostEstimate(
            flops=COST * repeats * width * rows * rows,
            bytes_accessed=12 * 2**20,
            transcendentals=0,
        ),
        name="attend_back",
    )(kind, queries, pairs, upstream, low, high, index, lse, delta)


def local(
    tokens,
    attn_gain,
    query_weight,
    key_matrix,
    value_matrix,
    out_weight,
    mlp_gain,
    gate_weight,
    up_weight,
    down_weight,
    segment_ids,
    positions,
    cotangent,
):
    heads = lax.axis_size("head")
    blocks = lax.axis_size("blk")
    blk = lax.axis_index("blk")
    head = lax.axis_index("head")
    own_rows = tokens.shape[0]
    rows = own_rows * heads
    width = HEAD_WIDTH
    repeats = QUERY_HEADS_ALL // KEY_VALUE_HEADS
    query_cols = query_weight.shape[1]

    score_scale = 1.0 / math.sqrt(width)

    qkv = RingGather(jnp.concatenate([query_weight, key_matrix, value_matrix], axis=1))
    qkv.go()
    gate_mine, gate_other = halves(gate_weight, 1)
    gate_got = flip(gate_other, "blk", PAIR_BIT)
    tokens_y = flip(tokens, "head", 2)
    gains = gain_hop(jnp.stack([attn_gain, mlp_gain]), 1)
    gains, gate_got, segment_ids, positions = join([qkv], gains, gate_got, segment_ids, positions)

    qkv.go()
    gate_full = group_gather(place_half(gate_mine, gate_got))
    gains = gain_hop(gains, 2)
    segs = slots(segment_ids.reshape(blocks, heads, own_rows), head)
    poss = slots(positions.reshape(blocks, heads, own_rows), head)
    index = slots(jnp.arange(blocks * rows, dtype=jnp.int32).reshape(blocks, heads, own_rows), head)
    own_seg = lax.dynamic_index_in_dim(segs, blk, 0, False)
    own_pos = lax.dynamic_index_in_dim(poss, blk, 0, False)
    high = lax.dynamic_index_in_dim(index, blk, 0, False)
    low = jnp.sum((segment_ids[None, :] < own_seg[:, None]).astype(jnp.int32), axis=1)
    block_seg = segment_ids.reshape(blocks, rows)
    seg_first, seg_last = block_seg[:, 0], block_seg[:, -1]
    ids = jnp.arange(blocks, dtype=jnp.int32)
    some = (ids <= blk) & (seg_last >= seg_first[blk])
    every = (ids < blk) & (seg_first == seg_last[blk])
    kind = jnp.where(every, 1, jnp.where(some, 2, 0)).astype(jnp.int32)
    index = index.reshape(blocks, 1, rows)
    up_mine, up_other = halves(up_weight, 1)
    tokens_y, gains, low, own_pos, up_other = join([qkv], tokens_y, gains, low, own_pos, up_other)

    qkv.go()
    up_got = flip(up_other, "blk", PAIR_BIT)
    tokens_parts = head_rest(tokens, tokens_y)
    gains = gain_hop(gains, 4)
    for bit in (8, 16, 32):
        gains = gain_hop(gains, bit)
    tokens_all = head_all(*tokens_parts)
    source_all = tokens_all.astype(F32)
    inverse_all = norm_scale(source_all)
    table = rotary_table(own_pos, width)
    inverse_all, gains, up_got, cosine, sine = join([qkv], inverse_all, gains, up_got, *table)
    table = (cosine, sine)
    qkv.rest()

    qkv.go()
    up_full = group_gather(place_half(up_mine, up_got))
    gains = gains.astype(F32)
    gain_one, gain_two = gains[0], gains[1]
    normed_all = (source_all * inverse_all * gain_one).astype(BF)
    source = source_all[:own_rows]
    inverse_one = inverse_all[:own_rows]
    cot_y = flip(cotangent, "head", 2)
    normed_all, out_in = join([qkv], normed_all, out_weight.T)

    qkv_full = qkv.full()
    out = RingGather(out_in)
    out.go()
    pair_linear = simple_product(normed_all, qkv_full[:, query_cols:])
    pair = jnp.concatenate(
        [
            apply_rotary(pair_linear[:, :width], table, 1.0).astype(BF),
            pair_linear[:, width:].astype(BF),
        ],
        axis=1,
    )
    pair, cot_y, normed_low = join([out], pair, cot_y, normed_all)
    pairs = RingGather(pair)
    pairs.go()
    out.go()
    queries = (
        apply_rotary(simple_product(normed_low, qkv_full[:, :query_cols]), table, 1.0).astype(BF)
        * score_scale
    )
    down_mine, down_other = halves(down_weight, 0)
    down_mine, down_other = down_mine.T, down_other.T
    queries, down_mine, down_other = join([pairs, out], queries, down_mine, down_other)
    pairs.go()
    out.go()
    down_got = flip(down_other, "blk", PAIR_BIT)
    down_got = join([pairs, out], down_got)
    pairs.go()
    out.rest()
    out.go()
    down_full = group_gather(place_half(down_mine, down_got))
    cot_x = flip(cotangent, "blk", PAIR_BIT)
    cot_x = join([pairs, out], cot_x)
    pairs.rest()
    pairs.go()
    cot_far = wide_far(cot_y, cot_x)
    cot_y, cot_x, *cot_far = join([pairs], cot_y, cot_x, *cot_far)

    pairs_full = pairs.full()
    attn_full, lse = attend(
        kind, queries, pairs_full, low[:, None], high[:, None], index, repeats, width
    )
    attn_low = attn_full.astype(BF)
    kept, near = head_near(times_rows(attn_low, out.full()))
    kept, near = barrier(kept, near)
    kept, far = head_far(kept, near)
    cotangent_all = wide_rest(cotangent, cot_y, cot_x, cot_far)
    kept, far, cotangent_all = barrier(kept, far, cotangent_all)
    residual = source + kept + far.astype(F32)

    inverse_two = norm_scale(residual)
    normed_two = (residual * inverse_two * gain_two).astype(BF)
    near_y, near_x = barrier(*wide_near(normed_two))
    far_y, far_x = wide_far(near_y, near_x)
    trio = jnp.concatenate([normed_two, near_y, near_x], axis=0)
    far_y, far_x, trio, beside = barrier(far_y, far_x, trio, flip(trio, "head", 1))
    far = jnp.concatenate([far_y, far_x], axis=1)
    normed_two_all = jnp.concatenate([trio, beside, far, flip(far, "head", 1)], axis=0)
    gate_lin = simple_product(normed_two_all, gate_full)
    up_lin = simple_product(after(normed_two_all, gate_lin), up_full)
    sigmoid_gate = jax.nn.sigmoid(gate_lin)
    silu_gate = gate_lin * sigmoid_gate
    hidden = (silu_gate * up_lin).astype(BF)
    down_part = outer_sum(cotangent_all, hidden).astype(BF)
    down_sum = group_sum(down_part)
    hidden_grad = simple_product(after(cotangent_all, down_part), down_full)
    gate_act_grad = (
        hidden_grad * up_lin * sigmoid_gate * (1.0 + gate_lin * (1.0 - sigmoid_gate))
    ).astype(BF)
    up_act_grad = (hidden_grad * silu_gate).astype(BF)

    back = WideSum(
        (times_rows(gate_act_grad, gate_full) + times_rows(up_act_grad, up_full)).astype(BF)
    )
    gate_act_grad, up_act_grad, hidden = join([back], gate_act_grad, up_act_grad, hidden)
    sent = back.go_far()
    gate_part = outer_sum(normed_two_all, after(gate_act_grad, *sent)).astype(BF)
    hidden, up_act_grad, gate_part = join([back], hidden, up_act_grad, gate_part)
    gate_sum = group_sum(gate_part)
    sent = back.go_near()
    up_part = outer_sum(normed_two_all, after(up_act_grad, *sent)).astype(BF)
    hidden, up_part = join([back], hidden, up_part)
    up_sum = group_sum(up_part)
    normed_two_grad = back.total()
    residual_grad = cotangent.astype(F32) + norm_back(
        residual, gain_two, inverse_two, normed_two_grad
    )
    branch_grad = residual_grad.astype(BF)
    branch_y = flip(branch_grad, "head", 2)
    layer_part = times_rows(after(hidden, branch_grad), down_full).astype(BF)
    mlp_gain_part = jnp.sum(after(normed_two_grad, branch_grad) * residual * inverse_two, axis=0)
    branch_y, mlp_gain_part, layer_part = barrier(branch_y, mlp_gain_part, layer_part)
    branch_all = head_all(*head_rest(branch_grad, branch_y))
    attn_grad = simple_product(branch_all, out.full()).astype(BF)
    attn_grad, branch_all, layer_part = barrier(attn_grad, branch_all, layer_part)

    row_delta = jnp.stack(
        [
            jnp.sum(
                attn_grad[:, r * width : (r + 1) * width].astype(F32)
                * attn_full[:, r * width : (r + 1) * width],
                axis=1,
            )
            for r in range(repeats)
        ]
    ).reshape(repeats, 1, rows)
    query_rot_grad, pair_grad = attend_back(
        kind,
        queries,
        pairs_full,
        attn_grad,
        low[None, :],
        high[None, :],
        index.reshape(blocks, rows, 1),
        lse.reshape(repeats, 1, rows),
        row_delta,
        repeats,
        width,
    )
    layer = WideSum(layer_part)
    query_rot_grad, pair_grad = join([layer], query_rot_grad, pair_grad)
    pair_sum = RingSum(pair_grad)
    sent = pair_sum.go()
    layer.go_far()
    out_part = outer_sum(branch_all, after(attn_low, *sent)).astype(BF)
    out_sum = lax.psum_scatter(out_part, "blk", scatter_dimension=0, tiled=True)
    out_part = join([pair_sum, layer], out_part)
    sent = pair_sum.go()
    layer.go_near()
    query_lin_grad = apply_rotary(
        after(query_rot_grad, *sent) * score_scale, table, -1.0
    ).astype(BF)
    query_lin_grad = join([pair_sum, layer], query_lin_grad)
    sent = pair_sum.go()
    layer_out = (residual + layer.total()).astype(BF)
    layer_out = join([pair_sum], layer_out)
    pair_sum.rest()
    pair_sum.go()
    join([pair_sum])
    pair_total = pair_sum.total()
    pair_lin_grad = jnp.concatenate(
        [apply_rotary(pair_total[:, :width], table, -1.0), pair_total[:, width:]], axis=1
    ).astype(BF)
    lin_grad = jnp.concatenate([query_lin_grad, pair_lin_grad], axis=1)
    qkv_sum = RingSum(outer_sum(normed_all, lin_grad).astype(BF))
    sent = qkv_sum.go()
    lin_grad = after(lin_grad, *sent)
    normed_grad_part = times_rows(lin_grad, qkv_full)
    gain_part = jnp.sum(normed_grad_part * source_all * inverse_all, axis=0)
    kept, near = head_near(normed_grad_part)
    gain_grads = jnp.stack([gain_part, mlp_gain_part])
    gain_grads = gain_grads + flip(gain_grads, "head", 1)
    kept, near, gain_grads = join([qkv_sum], kept, near, gain_grads)
    qkv_sum.go()
    kept, far = head_far(kept, near)
    gain_grads = gain_grads + flip(gain_grads, "head", 2)
    kept, far, gain_grads = join([qkv_sum], kept, far, gain_grads)
    qkv_sum.go()
    bit = blocks // 2
    gain_grads = gain_back(gain_grads, bit)
    normed_grad = kept + far.astype(F32)
    tokens_grad = residual_grad + norm_back(source, gain_one, inverse_one, normed_grad)
    gain_grads, tokens_grad = join([qkv_sum], gain_grads, tokens_grad)
    qkv_sum.rest()
    qkv_sum.go()
    while bit > 1:
        bit //= 2
        gain_grads = gain_back(gain_grads, bit)
    down_grad = narrow_half(*send_half(down_sum)).T
    gate_grad = narrow_half(*send_half(gate_sum))
    up_grad = narrow_half(*send_half(up_sum))
    out_grad = out_sum.astype(F32).T
    join([qkv_sum])
    qkv_grad = qkv_sum.total()
    return (
        layer_out,
        tokens_grad,
        gain_grads[0],
        qkv_grad[:, :query_cols],
        qkv_grad[:, query_cols : query_cols + width],
        qkv_grad[:, query_cols + width :],
        out_grad,
        gain_grads[1],
        gate_grad,
        up_grad,
        down_grad,
    )


def solution(mesh):
    return jax.shard_map(
        local,
        mesh=mesh,
        in_specs=(
            P(("blk", "head"), None),
            P("blk"),
            P("blk", "head"),
            P("blk", "head"),
            P("blk", "head"),
            P("head", "blk"),
            P("blk"),
            P("blk", "head"),
            P("blk", "head"),
            P("head", "blk"),
            P(),
            P(),
            P(("blk", "head"), None),
        ),
        out_specs=(
            P(("blk", "head"), None),
            P(("blk", "head"), None),
            P("blk"),
            P("blk", "head"),
            P("blk", "head"),
            P("blk", "head"),
            P("head", "blk"),
            P("blk"),
            P("blk", "head"),
            P("blk", "head"),
            P("head", "blk"),
        ),
        check_vma=False,
    )
```

```python
import math

import jax
import jax.numpy as jnp
from jax import lax
from jax.experimental import pallas as pl
from jax.experimental.pallas import tpu as pltpu
from jax.sharding import PartitionSpec as P

QUERY_HEADS_ALL = 8
KEY_VALUE_HEADS = 4
HEAD_WIDTH = 256
SEQ = 4096

EPSILON = 1e-06
THETA_BASE = 1000042.0
MASKED = -1e30
PAIR_BIT = 1
BF = jnp.bfloat16
F32 = jnp.float32


def after(value, *deps):
    return lax.optimization_barrier((value, *deps))[0]


def cycle_order(count):
    return list(range(0, count, 2)) + list(range(count - 1, 0, -2))


def cycle_place(index, count):
    return jnp.where(index % 2 == 0, index // 2, count // 2 + (count - 1 - index) // 2)


def cycle_owner(place, count):
    place = lax.rem(place + 2 * count, count)
    return jnp.where(place < count // 2, 2 * place, 2 * (count - 1 - place) + 1)


def ring_routes(count):
    order = cycle_order(count)
    up = [(order[i], order[(i + 1) % count]) for i in range(count)]
    return up, [(b, a) for a, b in up]


def barrier(*values):
    return lax.optimization_barrier(values)


def join(movers, *values):
    flights = [mover.flight() for mover in movers]
    flat = [value for flight in flights for value in flight]
    done = lax.optimization_barrier((*flat, *values))
    place = 0
    for mover, flight in zip(movers, flights):
        mover.land(list(done[place : place + len(flight)]))
        place += len(flight)
    rest = done[place:]
    return rest[0] if len(rest) == 1 else rest


class RingGather:
    def __init__(self, shard):
        self.count = lax.axis_size("blk")
        self.me = lax.axis_index("blk")
        self.place = cycle_place(self.me, self.count)
        self.routes = ring_routes(self.count)
        self.shard = self.left = self.right = shard
        self.step = 0
        self.parts = []

    def go(self):
        self.step += 1
        half = self.shard.shape[0] // 2
        left, right = self.left, self.right
        if self.step == self.count // 2:
            left, right = left[:half], right[half:]
        self.left = lax.ppermute(left, "blk", self.routes[0])
        self.right = lax.ppermute(right, "blk", self.routes[1])

    def rest(self):
        while self.step < self.count // 2 - 1:
            self.go()
            join([self])

    def flight(self):
        return [self.left, self.right]

    def land(self, values):
        self.left, self.right = values
        self.parts.append((self.step, self.left, self.right))

    def full(self):
        rows = self.shard.shape[0]
        out = jnp.zeros((self.count * rows, *self.shard.shape[1:]), self.shard.dtype)
        out = lax.dynamic_update_slice_in_dim(out, self.shard, self.me * rows, 0)
        for step, left, right in self.parts:
            low = cycle_owner(self.place - step, self.count) * rows
            high = cycle_owner(self.place + step, self.count) * rows
            if step == self.count // 2:
                high = low + rows // 2
            out = lax.dynamic_update_slice_in_dim(out, left, low, 0)
            out = lax.dynamic_update_slice_in_dim(out, right, high, 0)
        return out


class RingSum:
    def __init__(self, blocks):
        self.count = lax.axis_size("blk")
        self.place = cycle_place(lax.axis_index("blk"), self.count)
        self.routes = ring_routes(self.count)
        self.blocks = blocks
        self.rows = blocks.shape[0] // self.count
        self.step = self.count // 2

    def part(self, offset):
        return lax.dynamic_slice_in_dim(
            self.blocks, cycle_owner(self.place + offset, self.count) * self.rows, self.rows, 0
        )

    def go(self):
        half = self.rows // 2
        if self.step == self.count // 2:
            far = self.part(self.step)
            left, right = far[:half], far[half:]
        else:
            low, high = self.part(self.step), self.part(-self.step)
            left, right = self.left.astype(F32), self.right.astype(F32)
            if self.step == self.count // 2 - 1:
                left = jnp.concatenate([(low[:half].astype(F32) + left).astype(BF), low[half:]])
                right = jnp.concatenate([high[:half], (high[half:].astype(F32) + right).astype(BF)])
            else:
                left = (low.astype(F32) + left).astype(BF)
                right = (high.astype(F32) + right).astype(BF)
        self.left = lax.ppermute(left, "blk", self.routes[0])
        self.right = lax.ppermute(right, "blk", self.routes[1])
        self.step -= 1
        return left, right

    def rest(self):
        while self.step > 1:
            self.go()
            join([self])

    def flight(self):
        return [self.left, self.right]

    def land(self, values):
        self.left, self.right = values

    def total(self):
        return self.part(0).astype(F32) + self.left.astype(F32) + self.right.astype(F32)


def flip(value, axis, bit):
    return lax.ppermute(value, axis, [(i, i ^ bit) for i in range(lax.axis_size(axis))])


def head_rest(rows, other):
    pair = jnp.concatenate([rows, other], axis=0)
    return rows, other, flip(pair, "head", 1)


def head_all(rows, other, beside):
    count = rows.shape[0]
    return jnp.concatenate([rows, beside[:count], other, beside[count:]], axis=0)


def head_near(partial):
    low = partial.astype(BF).reshape(2, 2, partial.shape[0] // 4, *partial.shape[1:])
    return low[:, 0], flip(low[:, 1], "head", 1)


def head_far(kept, near):
    pair = kept.astype(F32) + near.astype(F32)
    return pair[0], flip(pair[1].astype(BF), "head", 2)


def slots(values, head_index):
    values = values.reshape(values.shape[0], 2, 2, values.shape[-1])
    values = jnp.where(head_index % 2 == 1, values[:, :, ::-1], values)
    values = jnp.where(head_index // 2 == 1, values[:, ::-1], values)
    return values.reshape(values.shape[0], -1)


def gain_hop(gains, bit):
    if bit >= lax.axis_size("blk"):
        return gains
    me = lax.axis_index("blk")
    other = flip(gains, "blk", bit)
    low = jnp.concatenate([gains, other], axis=1)
    high = jnp.concatenate([other, gains], axis=1)
    return jnp.where((me // bit) % 2 == 0, low, high)


def gain_back(grads, bit):
    low, high = jnp.split(grads, 2, axis=1)
    upper = (lax.axis_index("blk") // bit) % 2 == 1
    return jnp.where(upper, high, low) + flip(jnp.where(upper, low, high), "blk", bit)


def rotary_table(token_pos, width):
    half_size = width // 2
    frequency = THETA_BASE ** (-2.0 * jnp.arange(half_size, dtype=F32) / width)
    angles = token_pos.astype(F32)[:, None] * frequency[None, :]
    return jnp.cos(angles), jnp.sin(angles)


def apply_rotary(values, table, direction):
    cosine, sine_part = table
    sine_part = sine_part * direction
    half = cosine.shape[1]
    out = []
    for start in range(0, values.shape[1], 2 * half):
        first = values[:, start : start + half]
        second = values[:, start + half : start + 2 * half]
        out += [first * cosine - second * sine_part, second * cosine + first * sine_part]
    return jnp.concatenate(out, axis=1)


def norm_scale(values):
    return lax.rsqrt(jnp.mean(values * values, axis=-1, keepdims=True) + EPSILON)


def norm_back(values, gain_vec, inverse, upstream):
    weighted = upstream * gain_vec
    inner_mean = jnp.mean(weighted * values, axis=-1, keepdims=True)
    return inverse * weighted - values * (inverse * inverse * inverse) * inner_mean


def simple_product(matrix_a, matrix_b):
    return jnp.dot(matrix_a, matrix_b, preferred_element_type=F32)


def outer_sum(matrix_a, matrix_b):
    return lax.dot_general(
        matrix_a, matrix_b, (((0,), (0,)), ((), ())), preferred_element_type=F32
    )


def times_rows(matrix_a, matrix_b):
    return lax.dot_general(
        matrix_a, matrix_b, (((1,), (1,)), ((), ())), preferred_element_type=F32
    )


def pair_side(blk):
    return jnp.where((blk & PAIR_BIT) != 0, 1, 0)


def halves(shard, axis, side=None):
    if side is None:
        side = pair_side(lax.axis_index("blk"))
    low, high = jnp.split(shard, 2, axis=axis)
    return jnp.where(side == 0, low, high), jnp.where(side == 0, high, low)


def plane_groups():
    count = lax.axis_size("blk")
    return [[i for i in range(count) if i & PAIR_BIT == side] for side in (0, PAIR_BIT)]


def group_gather(rows):
    return lax.all_gather(rows, "blk", axis=0, tiled=True, axis_index_groups=plane_groups())


def group_sum(partial):
    return lax.psum_scatter(
        partial.astype(BF),
        "blk",
        scatter_dimension=0,
        tiled=True,
        axis_index_groups=plane_groups(),
    )


def send_half(both):
    mine, other = halves(both, 0)
    return mine, flip(other, "blk", PAIR_BIT)


def narrow_half(mine, other):
    side = pair_side(lax.axis_index("blk"))
    mine, other = mine.astype(F32), other.astype(F32)
    return jnp.concatenate(
        [jnp.where(side == 0, mine, other), jnp.where(side == 0, other, mine)], axis=1
    )


def place_half(mine, other):
    side = pair_side(lax.axis_index("blk"))
    return jnp.concatenate(
        [jnp.where(side == 0, mine, other), jnp.where(side == 0, other, mine)], axis=0
    )


def wide_near(rows):
    return flip(rows, "head", 2), flip(rows, "blk", PAIR_BIT)


def wide_far(near_y, near_z):
    half = near_y.shape[1] // 2
    return flip(near_z[:, :half], "head", 2), flip(near_y[:, half:], "blk", PAIR_BIT)


def wide_rest(rows, near_y, near_z, far):
    far = jnp.concatenate(far, axis=1)
    trio = jnp.concatenate([rows, near_y, near_z], axis=0)
    return jnp.concatenate([trio, flip(trio, "head", 1), far, flip(far, "head", 1)], axis=0)


class WideSum:
    def __init__(self, partial):
        self.rows = partial.shape[0] // 8
        rows = self.rows
        self.far, self.trio = partial[6 * rows : 7 * rows], partial[: 3 * rows]
        self.moving = [
            flip(partial[7 * rows :], "head", 1),
            flip(partial[3 * rows : 6 * rows], "head", 1),
        ]

    def flight(self):
        return self.moving

    def land(self, values):
        self.moving = values

    def go_far(self):
        far = self.far.astype(F32) + self.moving[0].astype(F32)
        self.trio = self.trio.astype(F32) + self.moving[1].astype(F32)
        half = far.shape[1] // 2
        sent = far[:, :half].astype(BF), far[:, half:].astype(BF)
        self.moving = [flip(sent[0], "head", 2), flip(sent[1], "blk", PAIR_BIT)]
        return sent

    def go_near(self):
        rows, half = self.rows, self.trio.shape[1] // 2
        to_z, to_y = (value.astype(F32) for value in self.moving)
        near_y, near_z = self.trio[rows : 2 * rows], self.trio[2 * rows :]
        near_z = jnp.concatenate([near_z[:, :half] + to_z, near_z[:, half:]], axis=1)
        near_y = jnp.concatenate([near_y[:, :half], near_y[:, half:] + to_y], axis=1)
        sent = near_y.astype(BF), near_z.astype(BF)
        self.moving = [flip(sent[0], "head", 2), flip(sent[1], "blk", PAIR_BIT)]
        return sent

    def total(self):
        return self.trio[: self.rows] + self.moving[0].astype(F32) + self.moving[1].astype(F32)


CHUNK = 256
COST = 40


def contract(a, b, dim_a, dim_b):
    return lax.dot_general(
        a, b, (((dim_a,), (dim_b,)), ((), ())), preferred_element_type=F32
    )


def attend_kernel(repeats, width, kind, q_ref, kv_ref, low_ref, high_ref, index_ref, out_ref, lse_ref, acc, top, total):
    step = pl.program_id(0)
    rows = q_ref.shape[0]

    @pl.when(step == 0)
    def _():
        acc[...] = jnp.zeros_like(acc)
        top[...] = jnp.full_like(top, MASKED)
        total[...] = jnp.zeros_like(total)

    def block(masked):
        keys = kv_ref[:, :width]
        values = kv_ref[:, width:]
        for start in range(0, rows, CHUNK):
            part = pl.ds(start, CHUNK)
            if masked:
                index = index_ref[0]
                allowed = (index >= low_ref[part, :]) & (index <= high_ref[part, :])
            for r in range(repeats):
                cols = slice(r * width, (r + 1) * width)
                scores = contract(q_ref[part, cols], keys, 1, 1)
                if masked:
                    scores = jnp.where(allowed, scores, MASKED)
                old = top[r, part, :]
                new = jnp.maximum(old, jnp.max(scores, axis=1, keepdims=True))
                probs = jnp.exp(scores - new)
                if masked:
                    probs = jnp.where(allowed, probs, 0.0)
                factor = jnp.exp(old - new)
                total[r, part, :] = total[r, part, :] * factor + jnp.sum(probs, axis=1, keepdims=True)
                top[r, part, :] = new
                acc[part, cols] = acc[part, cols] * factor + contract(probs.astype(BF), values, 1, 0)

    pl.when(kind[step] == 1)(lambda: block(False))
    pl.when(kind[step] == 2)(lambda: block(True))

    @pl.when(step == pl.num_programs(0) - 1)
    def _():
        for r in range(repeats):
            cols = slice(r * width, (r + 1) * width)
            out_ref[:, cols] = acc[:, cols] / total[r]
            lse_ref[r] = top[r] + jnp.log(total[r])


def attend(kind, queries, pairs, low, high, index, repeats, width):
    rows = queries.shape[0]
    blocks = pairs.shape[0] // rows
    whole = lambda shape: pl.BlockSpec(shape, lambda j, kind: (0,) * len(shape))
    return pl.pallas_call(
        lambda *refs: attend_kernel(repeats, width, *refs),
        grid_spec=pltpu.PrefetchScalarGridSpec(
            num_scalar_prefetch=1,
            grid=(blocks,),
            in_specs=[
                whole((rows, repeats * width)),
                pl.BlockSpec((rows, 2 * width), lambda j, kind: (j, 0)),
                whole((rows, 1)),
                whole((rows, 1)),
                pl.BlockSpec((1, 1, rows), lambda j, kind: (j, 0, 0)),
            ],
            out_specs=[whole((rows, repeats * width)), whole((repeats, rows, 1))],
            scratch_shapes=[
                pltpu.VMEM((rows, repeats * width), F32),
                pltpu.VMEM((repeats, rows, 1), F32),
                pltpu.VMEM((repeats, rows, 1), F32),
            ],
        ),
        out_shape=[
            jax.ShapeDtypeStruct((rows, repeats * width), F32),
            jax.ShapeDtypeStruct((repeats, rows, 1), F32),
        ],
        compiler_params=pltpu.CompilerParams(vmem_limit_bytes=40 * 2**20),
        cost_estimate=pl.CostEstimate(
            flops=COST * repeats * width * rows * rows,
            bytes_accessed=12 * 2**20,
            transcendentals=0,
        ),
        name="attend",
    )(kind, queries, pairs, low, high, index)


def attend_back_kernel(
    repeats, width, kind, q_ref, kv_ref, up_ref, low_ref, high_ref, index_ref, lse_ref, delta_ref, dq_ref, dkv_ref
):
    step = pl.program_id(0)
    rows = q_ref.shape[0]

    @pl.when(step == 0)
    def _():
        dq_ref[...] = jnp.zeros_like(dq_ref)

    def block(masked):
        for start in range(0, rows, CHUNK):
            part = pl.ds(start, CHUNK)
            keys = kv_ref[part, :width]
            values = kv_ref[part, width:]
            key_grad = jnp.zeros((CHUNK, width), F32)
            value_grad = jnp.zeros((CHUNK, width), F32)
            if masked:
                index = index_ref[0, part, :]
                allowed = (index >= low_ref[...]) & (index <= high_ref[...])
            for r in range(repeats):
                cols = slice(r * width, (r + 1) * width)
                queries, upstream = q_ref[:, cols], up_ref[:, cols]
                probs = jnp.exp(contract(keys, queries, 1, 1) - lse_ref[r])
                if masked:
                    probs = jnp.where(allowed, probs, 0.0)
                prob_grad = contract(values, upstream, 1, 1)
                score_grad = (probs * (prob_grad - delta_ref[r])).astype(BF)
                value_grad += contract(probs.astype(BF), upstream, 1, 0)
                key_grad += contract(score_grad, queries, 1, 0)
                dq_ref[:, cols] += contract(score_grad, keys, 0, 0)
            dkv_ref[part, :width] = key_grad.astype(BF)
            dkv_ref[part, width:] = value_grad.astype(BF)

    @pl.when(kind[step] == 0)
    def _():
        dkv_ref[...] = jnp.zeros_like(dkv_ref)

    pl.when(kind[step] == 1)(lambda: block(False))
    pl.when(kind[step] == 2)(lambda: block(True))


def attend_back(kind, queries, pairs, upstream, low, high, index, lse, delta, repeats, width):
    rows = queries.shape[0]
    blocks = pairs.shape[0] // rows
    whole = lambda shape: pl.BlockSpec(shape, lambda j, kind: (0,) * len(shape))
    return pl.pallas_call(
        lambda *refs: attend_back_kernel(repeats, width, *refs),
        grid_spec=pltpu.PrefetchScalarGridSpec(
            num_scalar_prefetch=1,
            grid=(blocks,),
            in_specs=[
                whole((rows, repeats * width)),
                pl.BlockSpec((rows, 2 * width), lambda j, kind: (j, 0)),
                whole((rows, repeats * width)),
                whole((1, rows)),
                whole((1, rows)),
                pl.BlockSpec((1, rows, 1), lambda j, kind: (j, 0, 0)),
                whole((repeats, 1, rows)),
                whole((repeats, 1, rows)),
            ],
            out_specs=[
                whole((rows, repeats * width)),
                pl.BlockSpec((rows, 2 * width), lambda j, kind: (j, 0)),
            ],
        ),
        out_shape=[
            jax.ShapeDtypeStruct((rows, repeats * width), F32),
            jax.ShapeDtypeStruct((blocks * rows, 2 * width), BF),
        ],
        compiler_params=pltpu.CompilerParams(vmem_limit_bytes=40 * 2**20),
        cost_estimate=pl.CostEstimate(
            flops=COST * repeats * width * rows * rows,
            bytes_accessed=12 * 2**20,
            transcendentals=0,
        ),
        name="attend_back",
    )(kind, queries, pairs, upstream, low, high, index, lse, delta)


def local(
    tokens,
    attn_gain,
    query_weight,
    key_matrix,
    value_matrix,
    out_weight,
    mlp_gain,
    gate_weight,
    up_weight,
    down_weight,
    segment_ids,
    positions,
    cotangent,
):
    heads = lax.axis_size("head")
    blocks = lax.axis_size("blk")
    blk = lax.axis_index("blk")
    head = lax.axis_index("head")
    own_rows = tokens.shape[0]
    rows = own_rows * heads
    width = HEAD_WIDTH
    repeats = QUERY_HEADS_ALL // KEY_VALUE_HEADS
    query_cols = query_weight.shape[1]

    score_scale = 1.0 / math.sqrt(width)

    projections = lax.all_gather(
        jnp.concatenate([query_weight, key_matrix, value_matrix, out_weight.T], axis=1),
        "blk",
        axis=0,
        tiled=True,
    )
    tokens_y = flip(tokens, "head", 2)
    side = pair_side(blk)
    gate_mine, gate_other = halves(gate_weight, 1, side)
    gate_got = flip(gate_other, "blk", PAIR_BIT)
    gains = gain_hop(jnp.stack([attn_gain, mlp_gain]), 1)
    gains = gain_hop(gains, 2)
    gains = gain_hop(gains, 4)
    for bit in (8, 16, 32):
        gains = gain_hop(gains, bit)
    tokens_y, gains, gate_got, gate_mine, segment_ids, positions = barrier(
        tokens_y, gains, gate_got, gate_mine, segment_ids, positions
    )
    gate_half = place_half(gate_mine, gate_got)
    tokens_parts = head_rest(tokens, tokens_y)
    segs = slots(segment_ids.reshape(blocks, heads, own_rows), head)
    poss = slots(positions.reshape(blocks, heads, own_rows), head)
    index = slots(jnp.arange(blocks * rows, dtype=jnp.int32).reshape(blocks, heads, own_rows), head)
    own_seg = lax.dynamic_index_in_dim(segs, blk, 0, False)
    own_pos = lax.dynamic_index_in_dim(poss, blk, 0, False)
    high = lax.dynamic_index_in_dim(index, blk, 0, False)
    low = jnp.sum((segment_ids[None, :] < own_seg[:, None]).astype(jnp.int32), axis=1)
    block_seg = segment_ids.reshape(blocks, rows)
    seg_first, seg_last = block_seg[:, 0], block_seg[:, -1]
    ids = jnp.arange(blocks, dtype=jnp.int32)
    some = (ids <= blk) & (seg_last >= seg_first[blk])
    every = (ids < blk) & (seg_first == seg_last[blk])
    kind = jnp.where(every, 1, jnp.where(some, 2, 0)).astype(jnp.int32)
    index = index.reshape(blocks, 1, rows)
    up_mine, up_other = halves(up_weight, 1, side)
    up_got = flip(up_other, "blk", PAIR_BIT)
    tokens_all = head_all(*tokens_parts)
    source_all = tokens_all.astype(F32)
    inverse_all = norm_scale(source_all)
    gains = gains.astype(F32)
    gain_one, gain_two = gains[0], gains[1]
    normed_all = (source_all * inverse_all * gain_one).astype(BF)
    source = source_all[:own_rows]
    inverse_one = inverse_all[:own_rows]
    table = rotary_table(own_pos, width)
    normed_all, low, up_mine, up_got, gate_half, cosine, sine = barrier(
        normed_all, low, up_mine, up_got, gate_half, *table
    )
    table = (cosine, sine)
    up_half = place_half(up_mine, up_got)
    down_mine, down_other = halves(down_weight, 0, side)
    down_mine, down_other = down_mine.T, down_other.T
    down_got = flip(down_other, "blk", PAIR_BIT)
    cot_y = flip(cotangent, "head", 2)
    normed_all, projections, up_half, down_mine, down_got, cot_y = barrier(
        normed_all, projections, up_half, down_mine, down_got, cot_y
    )
    qkv_full = projections[:, : query_cols + 2 * width]
    out_full = projections[:, query_cols + 2 * width :]
    gate_full = group_gather(gate_half)

    pair_linear = simple_product(normed_all, qkv_full[:, query_cols:])
    pair = jnp.concatenate(
        [
            apply_rotary(pair_linear[:, :width], table, 1.0).astype(BF),
            pair_linear[:, width:].astype(BF),
        ],
        axis=1,
    )
    pair, cot_y, normed_low, up_half = barrier(pair, cot_y, normed_all, up_half)
    up_full = group_gather(up_half)
    pairs = RingGather(pair)
    pairs.go()
    queries = (
        apply_rotary(simple_product(normed_low, qkv_full[:, :query_cols]), table, 1.0).astype(BF)
        * score_scale
    )
    queries = join([pairs], queries)
    pairs.go()
    join([pairs])
    pairs.go()
    down_full = group_gather(place_half(down_mine, down_got))
    cot_x = flip(cotangent, "blk", PAIR_BIT)
    cot_x, gate_full = join([pairs], cot_x, gate_full)
    pairs.rest()
    pairs.go()
    cot_far = wide_far(cot_y, cot_x)
    cot_y, cot_x, *cot_far = join([pairs], cot_y, cot_x, *cot_far)

    pairs_full = pairs.full()
    attn_full, lse = attend(
        kind, queries, pairs_full, low[:, None], high[:, None], index, repeats, width
    )
    attn_low = attn_full.astype(BF)
    kept, near = head_near(times_rows(attn_low, out_full))
    kept, near = barrier(kept, near)
    kept, far = head_far(kept, near)
    cotangent_all = wide_rest(cotangent, cot_y, cot_x, cot_far)
    kept, far, cotangent_all, up_full = barrier(kept, far, cotangent_all, up_full)
    residual = source + kept + far.astype(F32)

    inverse_two = norm_scale(residual)
    normed_two = (residual * inverse_two * gain_two).astype(BF)
    near_y, near_x = barrier(*wide_near(normed_two))
    far_y, far_x = wide_far(near_y, near_x)
    trio = jnp.concatenate([normed_two, near_y, near_x], axis=0)
    far_y, far_x, trio, beside, down_full = barrier(
        far_y, far_x, trio, flip(trio, "head", 1), down_full
    )
    far = jnp.concatenate([far_y, far_x], axis=1)
    normed_two_all = jnp.concatenate([trio, beside, far, flip(far, "head", 1)], axis=0)
    gate_lin = simple_product(normed_two_all, gate_full)
    up_lin = simple_product(after(normed_two_all, gate_lin), up_full)
    sigmoid_gate = jax.nn.sigmoid(gate_lin)
    silu_gate = gate_lin * sigmoid_gate
    hidden = (silu_gate * up_lin).astype(BF)
    down_part = outer_sum(cotangent_all, hidden).astype(BF)
    down_sum = group_sum(down_part)
    hidden_grad = simple_product(after(cotangent_all, down_part), down_full)
    gate_act_grad = (
        hidden_grad * up_lin * sigmoid_gate * (1.0 + gate_lin * (1.0 - sigmoid_gate))
    ).astype(BF)
    up_act_grad = (hidden_grad * silu_gate).astype(BF)

    back = WideSum(
        (times_rows(gate_act_grad, gate_full) + times_rows(up_act_grad, up_full)).astype(BF)
    )
    gate_act_grad, up_act_grad, hidden = join([back], gate_act_grad, up_act_grad, hidden)
    sent = back.go_far()
    gate_part = outer_sum(normed_two_all, after(gate_act_grad, *sent)).astype(BF)
    hidden, up_act_grad, gate_part = join([back], hidden, up_act_grad, gate_part)
    gate_sum = group_sum(gate_part)
    sent = back.go_near()
    up_part = outer_sum(normed_two_all, after(up_act_grad, *sent)).astype(BF)
    hidden, up_part = join([back], hidden, up_part)
    up_sum = group_sum(up_part)
    normed_two_grad = back.total()
    residual_grad = cotangent.astype(F32) + norm_back(
        residual, gain_two, inverse_two, normed_two_grad
    )
    branch_grad = residual_grad.astype(BF)
    branch_y = flip(branch_grad, "head", 2)
    layer_part = times_rows(after(hidden, branch_grad), down_full).astype(BF)
    mlp_gain_part = jnp.sum(after(normed_two_grad, branch_grad) * residual * inverse_two, axis=0)
    branch_y, mlp_gain_part, layer_part = barrier(branch_y, mlp_gain_part, layer_part)
    branch_all = head_all(*head_rest(branch_grad, branch_y))
    attn_grad = simple_product(branch_all, out_full).astype(BF)
    attn_grad, branch_all, layer_part = barrier(attn_grad, branch_all, layer_part)

    row_delta = jnp.stack(
        [
            jnp.sum(
                attn_grad[:, r * width : (r + 1) * width].astype(F32)
                * attn_full[:, r * width : (r + 1) * width],
                axis=1,
            )
            for r in range(repeats)
        ]
    ).reshape(repeats, 1, rows)
    query_rot_grad, pair_grad = attend_back(
        kind,
        queries,
        pairs_full,
        attn_grad,
        low[None, :],
        high[None, :],
        index.reshape(blocks, rows, 1),
        lse.reshape(repeats, 1, rows),
        row_delta,
        repeats,
        width,
    )
    layer = WideSum(layer_part)
    query_rot_grad, pair_grad = join([layer], query_rot_grad, pair_grad)
    pair_sum = RingSum(pair_grad)
    sent = pair_sum.go()
    layer.go_far()
    out_part = outer_sum(branch_all, after(attn_low, *sent)).astype(BF)
    out_sum = lax.psum_scatter(out_part, "blk", scatter_dimension=0, tiled=True)
    down_mine, down_other = send_half(down_sum)
    out_part, down_mine, down_other = join([pair_sum, layer], out_part, down_mine, down_other)
    sent = pair_sum.go()
    layer.go_near()
    query_lin_grad = apply_rotary(
        after(query_rot_grad, *sent) * score_scale, table, -1.0
    ).astype(BF)
    down_grad = narrow_half(after(down_mine, *sent), down_other).T
    gate_mine, gate_other = send_half(gate_sum)
    query_lin_grad, down_grad, gate_mine, gate_other = join(
        [pair_sum, layer], query_lin_grad, down_grad, gate_mine, gate_other
    )
    sent = pair_sum.go()
    layer_out = (residual + layer.total()).astype(BF)
    gate_grad = narrow_half(after(gate_mine, *sent), gate_other)
    layer_out, gate_grad = join([pair_sum], layer_out, gate_grad)
    pair_sum.rest()
    pair_sum.go()
    up_mine, up_other = join([pair_sum], *send_half(up_sum))
    pair_total = pair_sum.total()
    pair_lin_grad = jnp.concatenate(
        [apply_rotary(pair_total[:, :width], table, -1.0), pair_total[:, width:]], axis=1
    ).astype(BF)
    lin_grad = jnp.concatenate([query_lin_grad, pair_lin_grad], axis=1)
    qkv_sum = RingSum(outer_sum(normed_all, lin_grad).astype(BF))
    sent = qkv_sum.go()
    lin_grad = after(lin_grad, *sent)
    normed_grad_part = times_rows(lin_grad, qkv_full)
    gain_part = jnp.sum(normed_grad_part * source_all * inverse_all, axis=0)
    kept, near = head_near(normed_grad_part)
    gain_grads = jnp.stack([gain_part, mlp_gain_part])
    gain_grads = gain_grads + flip(gain_grads, "head", 1)
    kept, near, gain_grads = join([qkv_sum], kept, near, gain_grads)
    qkv_sum.go()
    kept, far = head_far(kept, near)
    gain_grads = gain_grads + flip(gain_grads, "head", 2)
    kept, far, gain_grads, out_sum = join([qkv_sum], kept, far, gain_grads, out_sum)
    qkv_sum.go()
    bit = blocks // 2
    gain_grads = gain_back(gain_grads, bit)
    normed_grad = kept + far.astype(F32)
    tokens_grad = residual_grad + norm_back(source, gain_one, inverse_one, normed_grad)
    out_grad = out_sum.astype(F32).T
    gain_grads, tokens_grad, out_grad = join([qkv_sum], gain_grads, tokens_grad, out_grad)
    qkv_sum.rest()
    qkv_sum.go()
    while bit > 1:
        bit //= 2
        gain_grads = gain_back(gain_grads, bit)
    up_grad = narrow_half(up_mine, up_other)
    join([qkv_sum])
    qkv_grad = qkv_sum.total()
    return (
        layer_out,
        tokens_grad,
        gain_grads[0],
        qkv_grad[:, :query_cols],
        qkv_grad[:, query_cols : query_cols + width],
        qkv_grad[:, query_cols + width :],
        out_grad,
        gain_grads[1],
        gate_grad,
        up_grad,
        down_grad,
    )


def solution(mesh):
    return jax.shard_map(
        local,
        mesh=mesh,
        in_specs=(
            P(("blk", "head"), None),
            P("blk"),
            P("blk", "head"),
            P("blk", "head"),
            P("blk", "head"),
            P("head", "blk"),
            P("blk"),
            P("blk", "head"),
            P("blk", "head"),
            P("head", "blk"),
            P(),
            P(),
            P(("blk", "head"), None),
        ),
        out_specs=(
            P(("blk", "head"), None),
            P(("blk", "head"), None),
            P("blk"),
            P("blk", "head"),
            P("blk", "head"),
            P("blk", "head"),
            P("head", "blk"),
            P("blk"),
            P("blk", "head"),
            P("blk", "head"),
            P("head", "blk"),
        ),
        check_vma=False,
    )
```

```python
import math

import jax
import jax.numpy as jnp
from jax import lax
from jax.experimental import pallas as pl
from jax.experimental.pallas import tpu as pltpu
from jax.sharding import PartitionSpec as P

QUERY_HEADS_ALL = 8
KEY_VALUE_HEADS = 4
HEAD_WIDTH = 256
SEQ = 4096

EPSILON = 1e-06
THETA_BASE = 1000042.0
MASKED = -1e30
PAIR_BIT = 1
BF = jnp.bfloat16
F32 = jnp.float32


def after(value, *deps):
    return lax.optimization_barrier((value, *deps))[0]


def cycle_order(count):
    return list(range(0, count, 2)) + list(range(count - 1, 0, -2))


def cycle_place(index, count):
    return jnp.where(index % 2 == 0, index // 2, count // 2 + (count - 1 - index) // 2)


def cycle_owner(place, count):
    place = lax.rem(place + 2 * count, count)
    return jnp.where(place < count // 2, 2 * place, 2 * (count - 1 - place) + 1)


def ring_routes(count):
    order = cycle_order(count)
    up = [(order[i], order[(i + 1) % count]) for i in range(count)]
    return up, [(b, a) for a, b in up]


def barrier(*values):
    return lax.optimization_barrier(values)


def join(movers, *values):
    flights = [mover.flight() for mover in movers]
    flat = [value for flight in flights for value in flight]
    done = lax.optimization_barrier((*flat, *values))
    place = 0
    for mover, flight in zip(movers, flights):
        mover.land(list(done[place : place + len(flight)]))
        place += len(flight)
    rest = done[place:]
    return rest[0] if len(rest) == 1 else rest


class RingGather:
    def __init__(self, shard):
        self.count = lax.axis_size("blk")
        self.me = lax.axis_index("blk")
        self.place = cycle_place(self.me, self.count)
        self.routes = ring_routes(self.count)
        self.shard = self.left = self.right = shard
        self.step = 0
        self.parts = []

    def go(self):
        self.step += 1
        half = self.shard.shape[0] // 2
        left, right = self.left, self.right
        if self.step == self.count // 2:
            left, right = left[:half], right[half:]
        self.left = lax.ppermute(left, "blk", self.routes[0])
        self.right = lax.ppermute(right, "blk", self.routes[1])

    def rest(self):
        while self.step < self.count // 2 - 1:
            self.go()
            join([self])

    def flight(self):
        return [self.left, self.right]

    def land(self, values):
        self.left, self.right = values
        self.parts.append((self.step, self.left, self.right))

    def full(self):
        rows = self.shard.shape[0]
        out = jnp.zeros((self.count * rows, *self.shard.shape[1:]), self.shard.dtype)
        out = lax.dynamic_update_slice_in_dim(out, self.shard, self.me * rows, 0)
        for step, left, right in self.parts:
            low = cycle_owner(self.place - step, self.count) * rows
            high = cycle_owner(self.place + step, self.count) * rows
            if step == self.count // 2:
                high = low + rows // 2
            out = lax.dynamic_update_slice_in_dim(out, left, low, 0)
            out = lax.dynamic_update_slice_in_dim(out, right, high, 0)
        return out


class RingSum:
    def __init__(self, blocks):
        self.count = lax.axis_size("blk")
        self.place = cycle_place(lax.axis_index("blk"), self.count)
        self.routes = ring_routes(self.count)
        self.blocks = blocks
        self.rows = blocks.shape[0] // self.count
        self.step = self.count // 2

    def part(self, offset):
        return lax.dynamic_slice_in_dim(
            self.blocks, cycle_owner(self.place + offset, self.count) * self.rows, self.rows, 0
        )

    def go(self):
        half = self.rows // 2
        if self.step == self.count // 2:
            far = self.part(self.step)
            left, right = far[:half], far[half:]
        else:
            low, high = self.part(self.step), self.part(-self.step)
            left, right = self.left.astype(F32), self.right.astype(F32)
            if self.step == self.count // 2 - 1:
                left = jnp.concatenate([(low[:half].astype(F32) + left).astype(BF), low[half:]])
                right = jnp.concatenate([high[:half], (high[half:].astype(F32) + right).astype(BF)])
            else:
                left = (low.astype(F32) + left).astype(BF)
                right = (high.astype(F32) + right).astype(BF)
        self.left = lax.ppermute(left, "blk", self.routes[0])
        self.right = lax.ppermute(right, "blk", self.routes[1])
        self.step -= 1
        return left, right

    def rest(self):
        while self.step > 1:
            self.go()
            join([self])

    def flight(self):
        return [self.left, self.right]

    def land(self, values):
        self.left, self.right = values

    def total(self):
        return self.part(0).astype(F32) + self.left.astype(F32) + self.right.astype(F32)


def flip(value, axis, bit):
    return lax.ppermute(value, axis, [(i, i ^ bit) for i in range(lax.axis_size(axis))])


def head_rest(rows, other):
    pair = jnp.concatenate([rows, other], axis=0)
    return rows, other, flip(pair, "head", 1)


def head_all(rows, other, beside):
    count = rows.shape[0]
    return jnp.concatenate([rows, beside[:count], other, beside[count:]], axis=0)


def head_near(partial):
    low = partial.astype(BF).reshape(2, 2, partial.shape[0] // 4, *partial.shape[1:])
    return low[:, 0], flip(low[:, 1], "head", 1)


def head_far(kept, near):
    pair = kept.astype(F32) + near.astype(F32)
    return pair[0], flip(pair[1].astype(BF), "head", 2)


def slots(values, head_index):
    values = values.reshape(values.shape[0], 2, 2, values.shape[-1])
    values = jnp.where(head_index % 2 == 1, values[:, :, ::-1], values)
    values = jnp.where(head_index // 2 == 1, values[:, ::-1], values)
    return values.reshape(values.shape[0], -1)


def gain_hop(gains, bit):
    if bit >= lax.axis_size("blk"):
        return gains
    me = lax.axis_index("blk")
    other = flip(gains, "blk", bit)
    low = jnp.concatenate([gains, other], axis=1)
    high = jnp.concatenate([other, gains], axis=1)
    return jnp.where((me // bit) % 2 == 0, low, high)


def gain_back(grads, bit):
    low, high = jnp.split(grads, 2, axis=1)
    upper = (lax.axis_index("blk") // bit) % 2 == 1
    return jnp.where(upper, high, low) + flip(jnp.where(upper, low, high), "blk", bit)


def rotary_table(token_pos, width):
    half_size = width // 2
    frequency = THETA_BASE ** (-2.0 * jnp.arange(half_size, dtype=F32) / width)
    angles = token_pos.astype(F32)[:, None] * frequency[None, :]
    return jnp.cos(angles), jnp.sin(angles)


def apply_rotary(values, table, direction):
    cosine, sine_part = table
    sine_part = sine_part * direction
    half = cosine.shape[1]
    out = []
    for start in range(0, values.shape[1], 2 * half):
        first = values[:, start : start + half]
        second = values[:, start + half : start + 2 * half]
        out += [first * cosine - second * sine_part, second * cosine + first * sine_part]
    return jnp.concatenate(out, axis=1)


def norm_scale(values):
    return lax.rsqrt(jnp.mean(values * values, axis=-1, keepdims=True) + EPSILON)


def norm_back(values, gain_vec, inverse, upstream):
    weighted = upstream * gain_vec
    inner_mean = jnp.mean(weighted * values, axis=-1, keepdims=True)
    return inverse * weighted - values * (inverse * inverse * inverse) * inner_mean


def simple_product(matrix_a, matrix_b):
    return jnp.dot(matrix_a, matrix_b, preferred_element_type=F32)


def outer_sum(matrix_a, matrix_b):
    return lax.dot_general(
        matrix_a, matrix_b, (((0,), (0,)), ((), ())), preferred_element_type=F32
    )


def times_rows(matrix_a, matrix_b):
    return lax.dot_general(
        matrix_a, matrix_b, (((1,), (1,)), ((), ())), preferred_element_type=F32
    )


def pair_side(blk):
    return jnp.where((blk & PAIR_BIT) != 0, 1, 0)


def halves(shard, axis, side=None):
    if side is None:
        side = pair_side(lax.axis_index("blk"))
    low, high = jnp.split(shard, 2, axis=axis)
    return jnp.where(side == 0, low, high), jnp.where(side == 0, high, low)


def plane_groups():
    count = lax.axis_size("blk")
    return [[i for i in range(count) if i & PAIR_BIT == side] for side in (0, PAIR_BIT)]


def group_gather(rows):
    return lax.all_gather(rows, "blk", axis=0, tiled=True, axis_index_groups=plane_groups())


def group_sum(partial):
    return lax.psum_scatter(
        partial.astype(BF),
        "blk",
        scatter_dimension=0,
        tiled=True,
        axis_index_groups=plane_groups(),
    )


def send_half(both):
    mine, other = halves(both, 0)
    return mine, flip(other, "blk", PAIR_BIT)


def narrow_half(mine, other):
    side = pair_side(lax.axis_index("blk"))
    mine, other = mine.astype(F32), other.astype(F32)
    return jnp.concatenate(
        [jnp.where(side == 0, mine, other), jnp.where(side == 0, other, mine)], axis=1
    )


def place_half(mine, other):
    side = pair_side(lax.axis_index("blk"))
    return jnp.concatenate(
        [jnp.where(side == 0, mine, other), jnp.where(side == 0, other, mine)], axis=0
    )


def wide_near(rows):
    return flip(rows, "head", 2), flip(rows, "blk", PAIR_BIT)


def wide_far(near_y, near_z):
    half = near_y.shape[1] // 2
    return flip(near_z[:, :half], "head", 2), flip(near_y[:, half:], "blk", PAIR_BIT)


def wide_rest(rows, near_y, near_z, far):
    far = jnp.concatenate(far, axis=1)
    trio = jnp.concatenate([rows, near_y, near_z], axis=0)
    return jnp.concatenate([trio, flip(trio, "head", 1), far, flip(far, "head", 1)], axis=0)


class WideSum:
    def __init__(self, partial):
        self.rows = partial.shape[0] // 8
        rows = self.rows
        self.far, self.trio = partial[6 * rows : 7 * rows], partial[: 3 * rows]
        self.moving = [
            flip(partial[7 * rows :], "head", 1),
            flip(partial[3 * rows : 6 * rows], "head", 1),
        ]

    def flight(self):
        return self.moving

    def land(self, values):
        self.moving = values

    def go_far(self):
        far = self.far.astype(F32) + self.moving[0].astype(F32)
        self.trio = self.trio.astype(F32) + self.moving[1].astype(F32)
        half = far.shape[1] // 2
        sent = far[:, :half].astype(BF), far[:, half:].astype(BF)
        self.moving = [flip(sent[0], "head", 2), flip(sent[1], "blk", PAIR_BIT)]
        return sent

    def go_near(self):
        rows, half = self.rows, self.trio.shape[1] // 2
        to_z, to_y = (value.astype(F32) for value in self.moving)
        near_y, near_z = self.trio[rows : 2 * rows], self.trio[2 * rows :]
        near_z = jnp.concatenate([near_z[:, :half] + to_z, near_z[:, half:]], axis=1)
        near_y = jnp.concatenate([near_y[:, :half], near_y[:, half:] + to_y], axis=1)
        sent = near_y.astype(BF), near_z.astype(BF)
        self.moving = [flip(sent[0], "head", 2), flip(sent[1], "blk", PAIR_BIT)]
        return sent

    def total(self):
        return self.trio[: self.rows] + self.moving[0].astype(F32) + self.moving[1].astype(F32)


CHUNK = 256
COST = 40


def contract(a, b, dim_a, dim_b):
    return lax.dot_general(
        a, b, (((dim_a,), (dim_b,)), ((), ())), preferred_element_type=F32
    )


def attend_kernel(repeats, width, kind, q_ref, kv_ref, low_ref, high_ref, index_ref, out_ref, lse_ref, acc, top, total):
    step = pl.program_id(0)
    rows = q_ref.shape[0]

    @pl.when(step == 0)
    def _():
        acc[...] = jnp.zeros_like(acc)
        top[...] = jnp.full_like(top, MASKED)
        total[...] = jnp.zeros_like(total)

    def block(masked):
        keys = kv_ref[:, :width]
        values = kv_ref[:, width:]
        for start in range(0, rows, CHUNK):
            part = pl.ds(start, CHUNK)
            if masked:
                index = index_ref[0]
                allowed = (index >= low_ref[part, :]) & (index <= high_ref[part, :])
            for r in range(repeats):
                cols = slice(r * width, (r + 1) * width)
                scores = contract(q_ref[part, cols], keys, 1, 1)
                if masked:
                    scores = jnp.where(allowed, scores, MASKED)
                old = top[r, part, :]
                new = jnp.maximum(old, jnp.max(scores, axis=1, keepdims=True))
                probs = jnp.exp(scores - new)
                if masked:
                    probs = jnp.where(allowed, probs, 0.0)
                factor = jnp.exp(old - new)
                total[r, part, :] = total[r, part, :] * factor + jnp.sum(probs, axis=1, keepdims=True)
                top[r, part, :] = new
                acc[part, cols] = acc[part, cols] * factor + contract(probs.astype(BF), values, 1, 0)

    pl.when(kind[step] == 1)(lambda: block(False))
    pl.when(kind[step] == 2)(lambda: block(True))

    @pl.when(step == pl.num_programs(0) - 1)
    def _():
        for r in range(repeats):
            cols = slice(r * width, (r + 1) * width)
            out_ref[:, cols] = acc[:, cols] / total[r]
            lse_ref[r] = top[r] + jnp.log(total[r])


def attend(kind, queries, pairs, low, high, index, repeats, width):
    rows = queries.shape[0]
    blocks = pairs.shape[0] // rows
    whole = lambda shape: pl.BlockSpec(shape, lambda j, kind: (0,) * len(shape))
    return pl.pallas_call(
        lambda *refs: attend_kernel(repeats, width, *refs),
        grid_spec=pltpu.PrefetchScalarGridSpec(
            num_scalar_prefetch=1,
            grid=(blocks,),
            in_specs=[
                whole((rows, repeats * width)),
                pl.BlockSpec((rows, 2 * width), lambda j, kind: (j, 0)),
                whole((rows, 1)),
                whole((rows, 1)),
                pl.BlockSpec((1, 1, rows), lambda j, kind: (j, 0, 0)),
            ],
            out_specs=[whole((rows, repeats * width)), whole((repeats, rows, 1))],
            scratch_shapes=[
                pltpu.VMEM((rows, repeats * width), F32),
                pltpu.VMEM((repeats, rows, 1), F32),
                pltpu.VMEM((repeats, rows, 1), F32),
            ],
        ),
        out_shape=[
            jax.ShapeDtypeStruct((rows, repeats * width), F32),
            jax.ShapeDtypeStruct((repeats, rows, 1), F32),
        ],
        compiler_params=pltpu.CompilerParams(vmem_limit_bytes=40 * 2**20),
        cost_estimate=pl.CostEstimate(
            flops=COST * repeats * width * rows * rows,
            bytes_accessed=12 * 2**20,
            transcendentals=0,
        ),
        name="attend",
    )(kind, queries, pairs, low, high, index)


def attend_back_kernel(
    repeats, width, kind, q_ref, kv_ref, up_ref, low_ref, high_ref, index_ref, lse_ref, delta_ref, dq_ref, dkv_ref
):
    step = pl.program_id(0)
    rows = q_ref.shape[0]

    @pl.when(step == 0)
    def _():
        dq_ref[...] = jnp.zeros_like(dq_ref)

    def block(masked):
        for start in range(0, rows, CHUNK):
            part = pl.ds(start, CHUNK)
            keys = kv_ref[part, :width]
            values = kv_ref[part, width:]
            key_grad = jnp.zeros((CHUNK, width), F32)
            value_grad = jnp.zeros((CHUNK, width), F32)
            if masked:
                index = index_ref[0, part, :]
                allowed = (index >= low_ref[...]) & (index <= high_ref[...])
            for r in range(repeats):
                cols = slice(r * width, (r + 1) * width)
                queries, upstream = q_ref[:, cols], up_ref[:, cols]
                probs = jnp.exp(contract(keys, queries, 1, 1) - lse_ref[r])
                if masked:
                    probs = jnp.where(allowed, probs, 0.0)
                prob_grad = contract(values, upstream, 1, 1)
                score_grad = (probs * (prob_grad - delta_ref[r])).astype(BF)
                value_grad += contract(probs.astype(BF), upstream, 1, 0)
                key_grad += contract(score_grad, queries, 1, 0)
                dq_ref[:, cols] += contract(score_grad, keys, 0, 0)
            dkv_ref[part, :width] = key_grad.astype(BF)
            dkv_ref[part, width:] = value_grad.astype(BF)

    @pl.when(kind[step] == 0)
    def _():
        dkv_ref[...] = jnp.zeros_like(dkv_ref)

    pl.when(kind[step] == 1)(lambda: block(False))
    pl.when(kind[step] == 2)(lambda: block(True))


def attend_back(kind, queries, pairs, upstream, low, high, index, lse, delta, repeats, width):
    rows = queries.shape[0]
    blocks = pairs.shape[0] // rows
    whole = lambda shape: pl.BlockSpec(shape, lambda j, kind: (0,) * len(shape))
    return pl.pallas_call(
        lambda *refs: attend_back_kernel(repeats, width, *refs),
        grid_spec=pltpu.PrefetchScalarGridSpec(
            num_scalar_prefetch=1,
            grid=(blocks,),
            in_specs=[
                whole((rows, repeats * width)),
                pl.BlockSpec((rows, 2 * width), lambda j, kind: (j, 0)),
                whole((rows, repeats * width)),
                whole((1, rows)),
                whole((1, rows)),
                pl.BlockSpec((1, rows, 1), lambda j, kind: (j, 0, 0)),
                whole((repeats, 1, rows)),
                whole((repeats, 1, rows)),
            ],
            out_specs=[
                whole((rows, repeats * width)),
                pl.BlockSpec((rows, 2 * width), lambda j, kind: (j, 0)),
            ],
        ),
        out_shape=[
            jax.ShapeDtypeStruct((rows, repeats * width), F32),
            jax.ShapeDtypeStruct((blocks * rows, 2 * width), BF),
        ],
        compiler_params=pltpu.CompilerParams(vmem_limit_bytes=40 * 2**20),
        cost_estimate=pl.CostEstimate(
            flops=COST * repeats * width * rows * rows,
            bytes_accessed=12 * 2**20,
            transcendentals=0,
        ),
        name="attend_back",
    )(kind, queries, pairs, upstream, low, high, index, lse, delta)


def local(
    tokens,
    attn_gain,
    query_weight,
    key_matrix,
    value_matrix,
    out_weight,
    mlp_gain,
    gate_weight,
    up_weight,
    down_weight,
    segment_ids,
    positions,
    cotangent,
):
    heads = lax.axis_size("head")
    blocks = lax.axis_size("blk")
    blk = lax.axis_index("blk")
    head = lax.axis_index("head")
    own_rows = tokens.shape[0]
    rows = own_rows * heads
    width = HEAD_WIDTH
    repeats = QUERY_HEADS_ALL // KEY_VALUE_HEADS
    query_cols = query_weight.shape[1]

    score_scale = 1.0 / math.sqrt(width)

    projections = lax.all_gather(
        jnp.concatenate([query_weight, key_matrix, value_matrix, out_weight.T], axis=1),
        "blk",
        axis=0,
        tiled=True,
    )
    tokens_y = flip(tokens, "head", 2)
    side = pair_side(blk)
    gate_mine, gate_other = halves(gate_weight, 1, side)
    gate_got = flip(gate_other, "blk", PAIR_BIT)
    gains = gain_hop(jnp.stack([attn_gain, mlp_gain]), 1)
    gains = gain_hop(gains, 2)
    gains = gain_hop(gains, 4)
    for bit in (8, 16, 32):
        gains = gain_hop(gains, bit)
    tokens_y, gains, gate_got, gate_mine, segment_ids, positions = barrier(
        tokens_y, gains, gate_got, gate_mine, segment_ids, positions
    )
    gate_half = place_half(gate_mine, gate_got)
    tokens_parts = head_rest(tokens, tokens_y)
    segs = slots(segment_ids.reshape(blocks, heads, own_rows), head)
    poss = slots(positions.reshape(blocks, heads, own_rows), head)
    index = slots(jnp.arange(blocks * rows, dtype=jnp.int32).reshape(blocks, heads, own_rows), head)
    own_seg = lax.dynamic_index_in_dim(segs, blk, 0, False)
    own_pos = lax.dynamic_index_in_dim(poss, blk, 0, False)
    high = lax.dynamic_index_in_dim(index, blk, 0, False)
    low = jnp.sum((segment_ids[None, :] < own_seg[:, None]).astype(jnp.int32), axis=1)
    block_seg = segment_ids.reshape(blocks, rows)
    seg_first, seg_last = block_seg[:, 0], block_seg[:, -1]
    ids = jnp.arange(blocks, dtype=jnp.int32)
    some = (ids <= blk) & (seg_last >= seg_first[blk])
    every = (ids < blk) & (seg_first == seg_last[blk])
    kind = jnp.where(every, 1, jnp.where(some, 2, 0)).astype(jnp.int32)
    index = index.reshape(blocks, 1, rows)
    up_mine, up_other = halves(up_weight, 1, side)
    up_got = flip(up_other, "blk", PAIR_BIT)
    tokens_all = head_all(*tokens_parts)
    source_all = tokens_all.astype(F32)
    inverse_all = norm_scale(source_all)
    gains = gains.astype(F32)
    gain_one, gain_two = gains[0], gains[1]
    normed_all = (source_all * inverse_all * gain_one).astype(BF)
    source = source_all[:own_rows]
    inverse_one = inverse_all[:own_rows]
    table = rotary_table(own_pos, width)
    normed_all, low, up_mine, up_got, gate_half, cosine, sine = barrier(
        normed_all, low, up_mine, up_got, gate_half, *table
    )
    table = (cosine, sine)
    up_half = place_half(up_mine, up_got)
    down_mine, down_other = halves(down_weight, 0, side)
    down_mine, down_other = down_mine.T, down_other.T
    down_got = flip(down_other, "blk", PAIR_BIT)
    cot_y = flip(cotangent, "head", 2)
    normed_all, projections, up_half, down_mine, down_got, cot_y = barrier(
        normed_all, projections, up_half, down_mine, down_got, cot_y
    )
    qkv_full = projections[:, : query_cols + 2 * width]
    out_full = projections[:, query_cols + 2 * width :]
    gate_full = group_gather(gate_half)

    pair_linear = simple_product(normed_all, qkv_full[:, query_cols:])
    pair = jnp.concatenate(
        [
            apply_rotary(pair_linear[:, :width], table, 1.0).astype(BF),
            pair_linear[:, width:].astype(BF),
        ],
        axis=1,
    )
    up_down_half = jnp.concatenate([up_half, place_half(down_mine, down_got)], axis=1)
    pair, cot_y, normed_low, up_down_half = barrier(pair, cot_y, normed_all, up_down_half)
    up_down_full = group_gather(up_down_half)
    pairs = RingGather(pair)
    pairs.go()
    queries = (
        apply_rotary(simple_product(normed_low, qkv_full[:, :query_cols]), table, 1.0).astype(BF)
        * score_scale
    )
    queries = join([pairs], queries)
    pairs.go()
    join([pairs])
    pairs.go()
    cot_x = flip(cotangent, "blk", PAIR_BIT)
    cot_x, gate_full = join([pairs], cot_x, gate_full)
    pairs.rest()
    pairs.go()
    cot_far = wide_far(cot_y, cot_x)
    cot_y, cot_x, *cot_far = join([pairs], cot_y, cot_x, *cot_far)

    pairs_full = pairs.full()
    attn_full, lse = attend(
        kind, queries, pairs_full, low[:, None], high[:, None], index, repeats, width
    )
    attn_low = attn_full.astype(BF)
    kept, near = head_near(times_rows(attn_low, out_full))
    kept, near = barrier(kept, near)
    kept, far = head_far(kept, near)
    cotangent_all = wide_rest(cotangent, cot_y, cot_x, cot_far)
    kept, far, cotangent_all = barrier(kept, far, cotangent_all)
    residual = source + kept + far.astype(F32)

    inverse_two = norm_scale(residual)
    normed_two = (residual * inverse_two * gain_two).astype(BF)
    near_y, near_x = barrier(*wide_near(normed_two))
    far_y, far_x = wide_far(near_y, near_x)
    trio = jnp.concatenate([normed_two, near_y, near_x], axis=0)
    far_y, far_x, trio, beside = barrier(far_y, far_x, trio, flip(trio, "head", 1))
    far = jnp.concatenate([far_y, far_x], axis=1)
    normed_two_all = jnp.concatenate([trio, beside, far, flip(far, "head", 1)], axis=0)
    gate_lin = simple_product(normed_two_all, gate_full)
    gate_lin, normed_two_all, up_down_full = barrier(gate_lin, normed_two_all, up_down_full)
    half = up_down_full.shape[1] // 2
    up_full, down_full = up_down_full[:, :half], up_down_full[:, half:]
    up_lin = simple_product(normed_two_all, up_full)
    sigmoid_gate = jax.nn.sigmoid(gate_lin)
    silu_gate = gate_lin * sigmoid_gate
    hidden = (silu_gate * up_lin).astype(BF)
    down_part = outer_sum(cotangent_all, hidden).astype(BF)
    down_sum = group_sum(down_part)
    hidden_grad = simple_product(after(cotangent_all, down_part), down_full)
    gate_act_grad = (
        hidden_grad * up_lin * sigmoid_gate * (1.0 + gate_lin * (1.0 - sigmoid_gate))
    ).astype(BF)
    up_act_grad = (hidden_grad * silu_gate).astype(BF)

    back = WideSum(
        (times_rows(gate_act_grad, gate_full) + times_rows(up_act_grad, up_full)).astype(BF)
    )
    gate_act_grad, up_act_grad, hidden = join([back], gate_act_grad, up_act_grad, hidden)
    sent = back.go_far()
    gate_part = outer_sum(normed_two_all, after(gate_act_grad, *sent)).astype(BF)
    hidden, up_act_grad, gate_part = join([back], hidden, up_act_grad, gate_part)
    gate_sum = group_sum(gate_part)
    sent = back.go_near()
    up_part = outer_sum(normed_two_all, after(up_act_grad, *sent)).astype(BF)
    hidden, up_part = join([back], hidden, up_part)
    up_sum = group_sum(up_part)
    normed_two_grad = back.total()
    residual_grad = cotangent.astype(F32) + norm_back(
        residual, gain_two, inverse_two, normed_two_grad
    )
    branch_grad = residual_grad.astype(BF)
    branch_y = flip(branch_grad, "head", 2)
    layer_part = times_rows(after(hidden, branch_grad), down_full).astype(BF)
    mlp_gain_part = jnp.sum(after(normed_two_grad, branch_grad) * residual * inverse_two, axis=0)
    branch_y, mlp_gain_part, layer_part = barrier(branch_y, mlp_gain_part, layer_part)
    branch_all = head_all(*head_rest(branch_grad, branch_y))
    attn_grad = simple_product(branch_all, out_full).astype(BF)
    attn_grad, branch_all, layer_part = barrier(attn_grad, branch_all, layer_part)

    row_delta = jnp.stack(
        [
            jnp.sum(
                attn_grad[:, r * width : (r + 1) * width].astype(F32)
                * attn_full[:, r * width : (r + 1) * width],
                axis=1,
            )
            for r in range(repeats)
        ]
    ).reshape(repeats, 1, rows)
    query_rot_grad, pair_grad = attend_back(
        kind,
        queries,
        pairs_full,
        attn_grad,
        low[None, :],
        high[None, :],
        index.reshape(blocks, rows, 1),
        lse.reshape(repeats, 1, rows),
        row_delta,
        repeats,
        width,
    )
    layer = WideSum(layer_part)
    query_rot_grad, pair_grad = join([layer], query_rot_grad, pair_grad)
    pair_sum = RingSum(pair_grad)
    sent = pair_sum.go()
    layer.go_far()
    out_part = outer_sum(branch_all, after(attn_low, *sent)).astype(BF)
    out_sum = lax.psum_scatter(out_part, "blk", scatter_dimension=0, tiled=True)
    down_mine, down_other = send_half(down_sum)
    out_part, down_mine, down_other = join([pair_sum, layer], out_part, down_mine, down_other)
    sent = pair_sum.go()
    layer.go_near()
    query_lin_grad = apply_rotary(
        after(query_rot_grad, *sent) * score_scale, table, -1.0
    ).astype(BF)
    down_grad = narrow_half(after(down_mine, *sent), down_other).T
    gate_mine, gate_other = send_half(gate_sum)
    query_lin_grad, down_grad, gate_mine, gate_other = join(
        [pair_sum, layer], query_lin_grad, down_grad, gate_mine, gate_other
    )
    sent = pair_sum.go()
    layer_out = (residual + layer.total()).astype(BF)
    gate_grad = narrow_half(after(gate_mine, *sent), gate_other)
    layer_out, gate_grad = join([pair_sum], layer_out, gate_grad)
    pair_sum.rest()
    pair_sum.go()
    up_mine, up_other = join([pair_sum], *send_half(up_sum))
    pair_total = pair_sum.total()
    pair_lin_grad = jnp.concatenate(
        [apply_rotary(pair_total[:, :width], table, -1.0), pair_total[:, width:]], axis=1
    ).astype(BF)
    lin_grad = jnp.concatenate([query_lin_grad, pair_lin_grad], axis=1)
    qkv_sum = RingSum(outer_sum(normed_all, lin_grad).astype(BF))
    sent = qkv_sum.go()
    lin_grad = after(lin_grad, *sent)
    normed_grad_part = times_rows(lin_grad, qkv_full)
    gain_part = jnp.sum(normed_grad_part * source_all * inverse_all, axis=0)
    kept, near = head_near(normed_grad_part)
    gain_grads = jnp.stack([gain_part, mlp_gain_part])
    gain_grads = gain_grads + flip(gain_grads, "head", 1)
    kept, near, gain_grads = join([qkv_sum], kept, near, gain_grads)
    qkv_sum.go()
    kept, far = head_far(kept, near)
    gain_grads = gain_grads + flip(gain_grads, "head", 2)
    kept, far, gain_grads, out_sum = join([qkv_sum], kept, far, gain_grads, out_sum)
    qkv_sum.go()
    bit = blocks // 2
    gain_grads = gain_back(gain_grads, bit)
    normed_grad = kept + far.astype(F32)
    tokens_grad = residual_grad + norm_back(source, gain_one, inverse_one, normed_grad)
    out_grad = out_sum.astype(F32).T
    gain_grads, tokens_grad, out_grad = join([qkv_sum], gain_grads, tokens_grad, out_grad)
    qkv_sum.rest()
    qkv_sum.go()
    while bit > 1:
        bit //= 2
        gain_grads = gain_back(gain_grads, bit)
    up_grad = narrow_half(up_mine, up_other)
    join([qkv_sum])
    qkv_grad = qkv_sum.total()
    return (
        layer_out,
        tokens_grad,
        gain_grads[0],
        qkv_grad[:, :query_cols],
        qkv_grad[:, query_cols : query_cols + width],
        qkv_grad[:, query_cols + width :],
        out_grad,
        gain_grads[1],
        gate_grad,
        up_grad,
        down_grad,
    )


def solution(mesh):
    return jax.shard_map(
        local,
        mesh=mesh,
        in_specs=(
            P(("blk", "head"), None),
            P("blk"),
            P("blk", "head"),
            P("blk", "head"),
            P("blk", "head"),
            P("head", "blk"),
            P("blk"),
            P("blk", "head"),
            P("blk", "head"),
            P("head", "blk"),
            P(),
            P(),
            P(("blk", "head"), None),
        ),
        out_specs=(
            P(("blk", "head"), None),
            P(("blk", "head"), None),
            P("blk"),
            P("blk", "head"),
            P("blk", "head"),
            P("blk", "head"),
            P("head", "blk"),
            P("blk"),
            P("blk", "head"),
            P("blk", "head"),
            P("head", "blk"),
        ),
        check_vma=False,
    )
```

```python
import math

import jax
import jax.numpy as jnp
from jax import lax
from jax.experimental import pallas as pl
from jax.experimental.pallas import tpu as pltpu
from jax.sharding import PartitionSpec as P

QUERY_HEADS_ALL = 8
KEY_VALUE_HEADS = 4
HEAD_WIDTH = 256
SEQ = 4096

EPSILON = 1e-06
THETA_BASE = 1000042.0
MASKED = -1e30
PAIR_BIT = 1
BF = jnp.bfloat16
F32 = jnp.float32


def after(value, *deps):
    return lax.optimization_barrier((value, *deps))[0]


def cycle_order(count):
    return list(range(0, count, 2)) + list(range(count - 1, 0, -2))


def cycle_place(index, count):
    return jnp.where(index % 2 == 0, index // 2, count // 2 + (count - 1 - index) // 2)


def cycle_owner(place, count):
    place = lax.rem(place + 2 * count, count)
    return jnp.where(place < count // 2, 2 * place, 2 * (count - 1 - place) + 1)


def ring_routes(count):
    order = cycle_order(count)
    up = [(order[i], order[(i + 1) % count]) for i in range(count)]
    return up, [(b, a) for a, b in up]


def barrier(*values):
    return lax.optimization_barrier(values)


def join(movers, *values):
    flights = [mover.flight() for mover in movers]
    flat = [value for flight in flights for value in flight]
    done = lax.optimization_barrier((*flat, *values))
    place = 0
    for mover, flight in zip(movers, flights):
        mover.land(list(done[place : place + len(flight)]))
        place += len(flight)
    rest = done[place:]
    return rest[0] if len(rest) == 1 else rest


class RingGather:
    def __init__(self, shard):
        self.count = lax.axis_size("blk")
        self.me = lax.axis_index("blk")
        self.place = cycle_place(self.me, self.count)
        self.routes = ring_routes(self.count)
        self.shard = self.left = self.right = shard
        self.step = 0
        self.parts = []

    def go(self):
        self.step += 1
        half = self.shard.shape[0] // 2
        left, right = self.left, self.right
        if self.step == self.count // 2:
            left, right = left[:half], right[half:]
        self.left = lax.ppermute(left, "blk", self.routes[0])
        self.right = lax.ppermute(right, "blk", self.routes[1])

    def rest(self):
        while self.step < self.count // 2 - 1:
            self.go()
            join([self])

    def flight(self):
        return [self.left, self.right]

    def land(self, values):
        self.left, self.right = values
        self.parts.append((self.step, self.left, self.right))

    def full(self):
        rows = self.shard.shape[0]
        out = jnp.zeros((self.count * rows, *self.shard.shape[1:]), self.shard.dtype)
        out = lax.dynamic_update_slice_in_dim(out, self.shard, self.me * rows, 0)
        for step, left, right in self.parts:
            low = cycle_owner(self.place - step, self.count) * rows
            high = cycle_owner(self.place + step, self.count) * rows
            if step == self.count // 2:
                high = low + rows // 2
            out = lax.dynamic_update_slice_in_dim(out, left, low, 0)
            out = lax.dynamic_update_slice_in_dim(out, right, high, 0)
        return out


class RingSum:
    def __init__(self, blocks):
        self.count = lax.axis_size("blk")
        self.place = cycle_place(lax.axis_index("blk"), self.count)
        self.routes = ring_routes(self.count)
        self.blocks = blocks
        self.rows = blocks.shape[0] // self.count
        self.step = self.count // 2

    def part(self, offset):
        return lax.dynamic_slice_in_dim(
            self.blocks, cycle_owner(self.place + offset, self.count) * self.rows, self.rows, 0
        )

    def go(self):
        half = self.rows // 2
        if self.step == self.count // 2:
            far = self.part(self.step)
            left, right = far[:half], far[half:]
        else:
            low, high = self.part(self.step), self.part(-self.step)
            left, right = self.left.astype(F32), self.right.astype(F32)
            if self.step == self.count // 2 - 1:
                left = jnp.concatenate([(low[:half].astype(F32) + left).astype(BF), low[half:]])
                right = jnp.concatenate([high[:half], (high[half:].astype(F32) + right).astype(BF)])
            else:
                left = (low.astype(F32) + left).astype(BF)
                right = (high.astype(F32) + right).astype(BF)
        self.left = lax.ppermute(left, "blk", self.routes[0])
        self.right = lax.ppermute(right, "blk", self.routes[1])
        self.step -= 1
        return left, right

    def rest(self):
        while self.step > 1:
            self.go()
            join([self])

    def flight(self):
        return [self.left, self.right]

    def land(self, values):
        self.left, self.right = values

    def total(self):
        return self.part(0).astype(F32) + self.left.astype(F32) + self.right.astype(F32)


def flip(value, axis, bit):
    return lax.ppermute(value, axis, [(i, i ^ bit) for i in range(lax.axis_size(axis))])


def head_rest(rows, other):
    pair = jnp.concatenate([rows, other], axis=0)
    return rows, other, flip(pair, "head", 1)


def head_all(rows, other, beside):
    count = rows.shape[0]
    return jnp.concatenate([rows, beside[:count], other, beside[count:]], axis=0)


def head_near(partial):
    low = partial.astype(BF).reshape(2, 2, partial.shape[0] // 4, *partial.shape[1:])
    return low[:, 0], flip(low[:, 1], "head", 1)


def head_far(kept, near):
    pair = kept.astype(F32) + near.astype(F32)
    return pair[0], flip(pair[1].astype(BF), "head", 2)


def slots(values, head_index):
    values = values.reshape(values.shape[0], 2, 2, values.shape[-1])
    values = jnp.where(head_index % 2 == 1, values[:, :, ::-1], values)
    values = jnp.where(head_index // 2 == 1, values[:, ::-1], values)
    return values.reshape(values.shape[0], -1)


def gain_hop(gains, bit):
    if bit >= lax.axis_size("blk"):
        return gains
    me = lax.axis_index("blk")
    other = flip(gains, "blk", bit)
    low = jnp.concatenate([gains, other], axis=1)
    high = jnp.concatenate([other, gains], axis=1)
    return jnp.where((me // bit) % 2 == 0, low, high)


def gain_back(grads, bit):
    low, high = jnp.split(grads, 2, axis=1)
    upper = (lax.axis_index("blk") // bit) % 2 == 1
    return jnp.where(upper, high, low) + flip(jnp.where(upper, low, high), "blk", bit)


def rotary_table(token_pos, width):
    half_size = width // 2
    frequency = THETA_BASE ** (-2.0 * jnp.arange(half_size, dtype=F32) / width)
    angles = token_pos.astype(F32)[:, None] * frequency[None, :]
    return jnp.cos(angles), jnp.sin(angles)


def apply_rotary(values, table, direction):
    cosine, sine_part = table
    sine_part = sine_part * direction
    half = cosine.shape[1]
    out = []
    for start in range(0, values.shape[1], 2 * half):
        first = values[:, start : start + half]
        second = values[:, start + half : start + 2 * half]
        out += [first * cosine - second * sine_part, second * cosine + first * sine_part]
    return jnp.concatenate(out, axis=1)


def norm_scale(values):
    return lax.rsqrt(jnp.mean(values * values, axis=-1, keepdims=True) + EPSILON)


def norm_back(values, gain_vec, inverse, upstream):
    weighted = upstream * gain_vec
    inner_mean = jnp.mean(weighted * values, axis=-1, keepdims=True)
    return inverse * weighted - values * (inverse * inverse * inverse) * inner_mean


def simple_product(matrix_a, matrix_b):
    return jnp.dot(matrix_a, matrix_b, preferred_element_type=F32)


def outer_sum(matrix_a, matrix_b):
    return lax.dot_general(
        matrix_a, matrix_b, (((0,), (0,)), ((), ())), preferred_element_type=F32
    )


def times_rows(matrix_a, matrix_b):
    return lax.dot_general(
        matrix_a, matrix_b, (((1,), (1,)), ((), ())), preferred_element_type=F32
    )


def pair_side(blk):
    return jnp.where((blk & PAIR_BIT) != 0, 1, 0)


def halves(shard, axis, side=None):
    if side is None:
        side = pair_side(lax.axis_index("blk"))
    low, high = jnp.split(shard, 2, axis=axis)
    return jnp.where(side == 0, low, high), jnp.where(side == 0, high, low)


def plane_groups():
    count = lax.axis_size("blk")
    return [[i for i in range(count) if i & PAIR_BIT == side] for side in (0, PAIR_BIT)]


def group_gather(rows):
    return lax.all_gather(rows, "blk", axis=0, tiled=True, axis_index_groups=plane_groups())


def group_sum(partial):
    return lax.psum_scatter(
        partial.astype(BF),
        "blk",
        scatter_dimension=0,
        tiled=True,
        axis_index_groups=plane_groups(),
    )


def send_half(both):
    mine, other = halves(both, 0)
    return mine, flip(other, "blk", PAIR_BIT)


def narrow_half(mine, other):
    side = pair_side(lax.axis_index("blk"))
    mine, other = mine.astype(F32), other.astype(F32)
    return jnp.concatenate(
        [jnp.where(side == 0, mine, other), jnp.where(side == 0, other, mine)], axis=1
    )


def place_half(mine, other):
    side = pair_side(lax.axis_index("blk"))
    return jnp.concatenate(
        [jnp.where(side == 0, mine, other), jnp.where(side == 0, other, mine)], axis=0
    )


def wide_near(rows):
    return flip(rows, "head", 2), flip(rows, "blk", PAIR_BIT)


def wide_far(near_y, near_z):
    half = near_y.shape[1] // 2
    return flip(near_z[:, :half], "head", 2), flip(near_y[:, half:], "blk", PAIR_BIT)


def wide_rest(rows, near_y, near_z, far):
    far = jnp.concatenate(far, axis=1)
    trio = jnp.concatenate([rows, near_y, near_z], axis=0)
    return jnp.concatenate([trio, flip(trio, "head", 1), far, flip(far, "head", 1)], axis=0)


class WideSum:
    def __init__(self, partial):
        self.rows = partial.shape[0] // 8
        rows = self.rows
        self.far, self.trio = partial[6 * rows : 7 * rows], partial[: 3 * rows]
        self.moving = [
            flip(partial[7 * rows :], "head", 1),
            flip(partial[3 * rows : 6 * rows], "head", 1),
        ]

    def flight(self):
        return self.moving

    def land(self, values):
        self.moving = values

    def go_far(self):
        far = self.far.astype(F32) + self.moving[0].astype(F32)
        self.trio = self.trio.astype(F32) + self.moving[1].astype(F32)
        half = far.shape[1] // 2
        sent = far[:, :half].astype(BF), far[:, half:].astype(BF)
        self.moving = [flip(sent[0], "head", 2), flip(sent[1], "blk", PAIR_BIT)]
        return sent

    def go_near(self):
        rows, half = self.rows, self.trio.shape[1] // 2
        to_z, to_y = (value.astype(F32) for value in self.moving)
        near_y, near_z = self.trio[rows : 2 * rows], self.trio[2 * rows :]
        near_z = jnp.concatenate([near_z[:, :half] + to_z, near_z[:, half:]], axis=1)
        near_y = jnp.concatenate([near_y[:, :half], near_y[:, half:] + to_y], axis=1)
        sent = near_y.astype(BF), near_z.astype(BF)
        self.moving = [flip(sent[0], "head", 2), flip(sent[1], "blk", PAIR_BIT)]
        return sent

    def total(self):
        return self.trio[: self.rows] + self.moving[0].astype(F32) + self.moving[1].astype(F32)


CHUNK = 256
COST = 40


def contract(a, b, dim_a, dim_b):
    return lax.dot_general(
        a, b, (((dim_a,), (dim_b,)), ((), ())), preferred_element_type=F32
    )


def attend_kernel(repeats, width, kind, q_ref, kv_ref, low_ref, high_ref, index_ref, out_ref, lse_ref, acc, top, total):
    step = pl.program_id(0)
    rows = q_ref.shape[0]

    @pl.when(step == 0)
    def _():
        acc[...] = jnp.zeros_like(acc)
        top[...] = jnp.full_like(top, MASKED)
        total[...] = jnp.zeros_like(total)

    def block(masked):
        keys = kv_ref[:, :width]
        values = kv_ref[:, width:]
        for start in range(0, rows, CHUNK):
            part = pl.ds(start, CHUNK)
            if masked:
                index = index_ref[0]
                allowed = (index >= low_ref[part, :]) & (index <= high_ref[part, :])
            for r in range(repeats):
                cols = slice(r * width, (r + 1) * width)
                scores = contract(q_ref[part, cols], keys, 1, 1)
                if masked:
                    scores = jnp.where(allowed, scores, MASKED)
                old = top[r, part, :]
                new = jnp.maximum(old, jnp.max(scores, axis=1, keepdims=True))
                probs = jnp.exp(scores - new)
                if masked:
                    probs = jnp.where(allowed, probs, 0.0)
                factor = jnp.exp(old - new)
                total[r, part, :] = total[r, part, :] * factor + jnp.sum(probs, axis=1, keepdims=True)
                top[r, part, :] = new
                acc[part, cols] = acc[part, cols] * factor + contract(probs.astype(BF), values, 1, 0)

    pl.when(kind[step] == 1)(lambda: block(False))
    pl.when(kind[step] == 2)(lambda: block(True))

    @pl.when(step == pl.num_programs(0) - 1)
    def _():
        for r in range(repeats):
            cols = slice(r * width, (r + 1) * width)
            out_ref[:, cols] = acc[:, cols] / total[r]
            lse_ref[r] = top[r] + jnp.log(total[r])


def attend(kind, queries, pairs, low, high, index, repeats, width):
    rows = queries.shape[0]
    blocks = pairs.shape[0] // rows
    whole = lambda shape: pl.BlockSpec(shape, lambda j, kind: (0,) * len(shape))
    return pl.pallas_call(
        lambda *refs: attend_kernel(repeats, width, *refs),
        grid_spec=pltpu.PrefetchScalarGridSpec(
            num_scalar_prefetch=1,
            grid=(blocks,),
            in_specs=[
                whole((rows, repeats * width)),
                pl.BlockSpec((rows, 2 * width), lambda j, kind: (j, 0)),
                whole((rows, 1)),
                whole((rows, 1)),
                pl.BlockSpec((1, 1, rows), lambda j, kind: (j, 0, 0)),
            ],
            out_specs=[whole((rows, repeats * width)), whole((repeats, rows, 1))],
            scratch_shapes=[
                pltpu.VMEM((rows, repeats * width), F32),
                pltpu.VMEM((repeats, rows, 1), F32),
                pltpu.VMEM((repeats, rows, 1), F32),
            ],
        ),
        out_shape=[
            jax.ShapeDtypeStruct((rows, repeats * width), F32),
            jax.ShapeDtypeStruct((repeats, rows, 1), F32),
        ],
        compiler_params=pltpu.CompilerParams(vmem_limit_bytes=40 * 2**20),
        cost_estimate=pl.CostEstimate(
            flops=COST * repeats * width * rows * rows,
            bytes_accessed=12 * 2**20,
            transcendentals=0,
        ),
        name="attend",
    )(kind, queries, pairs, low, high, index)


def attend_back_kernel(
    repeats, width, kind, q_ref, kv_ref, up_ref, low_ref, high_ref, index_ref, lse_ref, delta_ref, dq_ref, dkv_ref
):
    step = pl.program_id(0)
    rows = q_ref.shape[0]

    @pl.when(step == 0)
    def _():
        dq_ref[...] = jnp.zeros_like(dq_ref)

    def block(masked):
        for start in range(0, rows, CHUNK):
            part = pl.ds(start, CHUNK)
            keys = kv_ref[part, :width]
            values = kv_ref[part, width:]
            key_grad = jnp.zeros((CHUNK, width), F32)
            value_grad = jnp.zeros((CHUNK, width), F32)
            if masked:
                index = index_ref[0, part, :]
                allowed = (index >= low_ref[...]) & (index <= high_ref[...])
            for r in range(repeats):
                cols = slice(r * width, (r + 1) * width)
                queries, upstream = q_ref[:, cols], up_ref[:, cols]
                probs = jnp.exp(contract(keys, queries, 1, 1) - lse_ref[r])
                if masked:
                    probs = jnp.where(allowed, probs, 0.0)
                prob_grad = contract(values, upstream, 1, 1)
                score_grad = (probs * (prob_grad - delta_ref[r])).astype(BF)
                value_grad += contract(probs.astype(BF), upstream, 1, 0)
                key_grad += contract(score_grad, queries, 1, 0)
                dq_ref[:, cols] += contract(score_grad, keys, 0, 0)
            dkv_ref[part, :width] = key_grad.astype(BF)
            dkv_ref[part, width:] = value_grad.astype(BF)

    @pl.when(kind[step] == 0)
    def _():
        dkv_ref[...] = jnp.zeros_like(dkv_ref)

    pl.when(kind[step] == 1)(lambda: block(False))
    pl.when(kind[step] == 2)(lambda: block(True))


def attend_back(kind, queries, pairs, upstream, low, high, index, lse, delta, repeats, width):
    rows = queries.shape[0]
    blocks = pairs.shape[0] // rows
    whole = lambda shape: pl.BlockSpec(shape, lambda j, kind: (0,) * len(shape))
    return pl.pallas_call(
        lambda *refs: attend_back_kernel(repeats, width, *refs),
        grid_spec=pltpu.PrefetchScalarGridSpec(
            num_scalar_prefetch=1,
            grid=(blocks,),
            in_specs=[
                whole((rows, repeats * width)),
                pl.BlockSpec((rows, 2 * width), lambda j, kind: (j, 0)),
                whole((rows, repeats * width)),
                whole((1, rows)),
                whole((1, rows)),
                pl.BlockSpec((1, rows, 1), lambda j, kind: (j, 0, 0)),
                whole((repeats, 1, rows)),
                whole((repeats, 1, rows)),
            ],
            out_specs=[
                whole((rows, repeats * width)),
                pl.BlockSpec((rows, 2 * width), lambda j, kind: (j, 0)),
            ],
        ),
        out_shape=[
            jax.ShapeDtypeStruct((rows, repeats * width), F32),
            jax.ShapeDtypeStruct((blocks * rows, 2 * width), BF),
        ],
        compiler_params=pltpu.CompilerParams(vmem_limit_bytes=40 * 2**20),
        cost_estimate=pl.CostEstimate(
            flops=COST * repeats * width * rows * rows,
            bytes_accessed=12 * 2**20,
            transcendentals=0,
        ),
        name="attend_back",
    )(kind, queries, pairs, upstream, low, high, index, lse, delta)


def local(
    tokens,
    attn_gain,
    query_weight,
    key_matrix,
    value_matrix,
    out_weight,
    mlp_gain,
    gate_weight,
    up_weight,
    down_weight,
    segment_ids,
    positions,
    cotangent,
):
    heads = lax.axis_size("head")
    blocks = lax.axis_size("blk")
    blk = lax.axis_index("blk")
    head = lax.axis_index("head")
    own_rows = tokens.shape[0]
    rows = own_rows * heads
    width = HEAD_WIDTH
    repeats = QUERY_HEADS_ALL // KEY_VALUE_HEADS
    query_cols = query_weight.shape[1]

    score_scale = 1.0 / math.sqrt(width)

    projections = lax.all_gather(
        jnp.concatenate([query_weight, key_matrix, value_matrix, out_weight.T], axis=1),
        "blk",
        axis=0,
        tiled=True,
    )
    tokens_y = flip(tokens, "head", 2)
    side = pair_side(blk)
    gate_mine, gate_other = halves(gate_weight, 1, side)
    gate_got = flip(gate_other, "blk", PAIR_BIT)
    gains = gain_hop(jnp.stack([attn_gain, mlp_gain]), 1)
    gains = gain_hop(gains, 2)
    gains = gain_hop(gains, 4)
    for bit in (8, 16, 32):
        gains = gain_hop(gains, bit)
    tokens_y, gains, gate_got, gate_mine, segment_ids, positions = barrier(
        tokens_y, gains, gate_got, gate_mine, segment_ids, positions
    )
    gate_half = place_half(gate_mine, gate_got)
    tokens_parts = head_rest(tokens, tokens_y)
    segs = slots(segment_ids.reshape(blocks, heads, own_rows), head)
    poss = slots(positions.reshape(blocks, heads, own_rows), head)
    index = slots(jnp.arange(blocks * rows, dtype=jnp.int32).reshape(blocks, heads, own_rows), head)
    own_seg = lax.dynamic_index_in_dim(segs, blk, 0, False)
    own_pos = lax.dynamic_index_in_dim(poss, blk, 0, False)
    high = lax.dynamic_index_in_dim(index, blk, 0, False)
    low = jnp.sum((segment_ids[None, :] < own_seg[:, None]).astype(jnp.int32), axis=1)
    block_seg = segment_ids.reshape(blocks, rows)
    seg_first, seg_last = block_seg[:, 0], block_seg[:, -1]
    ids = jnp.arange(blocks, dtype=jnp.int32)
    some = (ids <= blk) & (seg_last >= seg_first[blk])
    every = (ids < blk) & (seg_first == seg_last[blk])
    kind = jnp.where(every, 1, jnp.where(some, 2, 0)).astype(jnp.int32)
    index = index.reshape(blocks, 1, rows)
    up_mine, up_other = halves(up_weight, 1, side)
    up_got = flip(up_other, "blk", PAIR_BIT)
    tokens_all = head_all(*tokens_parts)
    source_all = tokens_all.astype(F32)
    inverse_all = norm_scale(source_all)
    gains = gains.astype(F32)
    gain_one, gain_two = gains[0], gains[1]
    normed_all = (source_all * inverse_all * gain_one).astype(BF)
    source = source_all[:own_rows]
    inverse_one = inverse_all[:own_rows]
    table = rotary_table(own_pos, width)
    normed_all, low, up_mine, up_got, gate_half, cosine, sine = barrier(
        normed_all, low, up_mine, up_got, gate_half, *table
    )
    table = (cosine, sine)
    up_half = place_half(up_mine, up_got)
    down_mine, down_other = halves(down_weight, 0, side)
    down_mine, down_other = down_mine.T, down_other.T
    down_got = flip(down_other, "blk", PAIR_BIT)
    cot_y = flip(cotangent, "head", 2)
    normed_all, projections, up_half, down_mine, down_got, cot_y = barrier(
        normed_all, projections, up_half, down_mine, down_got, cot_y
    )
    qkv_full = projections[:, : query_cols + 2 * width]
    out_full = projections[:, query_cols + 2 * width :]
    gate_full = group_gather(gate_half)

    pair_linear = simple_product(normed_all, qkv_full[:, query_cols:])
    pair = jnp.concatenate(
        [
            apply_rotary(pair_linear[:, :width], table, 1.0).astype(BF),
            pair_linear[:, width:].astype(BF),
        ],
        axis=1,
    )
    up_down_half = jnp.concatenate([up_half, place_half(down_mine, down_got)], axis=1)
    pair, cot_y, normed_low, up_down_half = barrier(pair, cot_y, normed_all, up_down_half)
    up_down_full = group_gather(up_down_half)
    pairs = RingGather(pair)
    pairs.go()
    queries = (
        apply_rotary(simple_product(normed_low, qkv_full[:, :query_cols]), table, 1.0).astype(BF)
        * score_scale
    )
    queries = join([pairs], queries)
    pairs.go()
    join([pairs])
    pairs.go()
    cot_x = flip(cotangent, "blk", PAIR_BIT)
    cot_x, gate_full = join([pairs], cot_x, gate_full)
    pairs.rest()
    pairs.go()
    cot_far = wide_far(cot_y, cot_x)
    cot_y, cot_x, *cot_far = join([pairs], cot_y, cot_x, *cot_far)

    pairs_full = pairs.full()
    attn_full, lse = attend(
        kind, queries, pairs_full, low[:, None], high[:, None], index, repeats, width
    )
    attn_low = attn_full.astype(BF)
    kept, near = head_near(times_rows(attn_low, out_full))
    kept, near = barrier(kept, near)
    kept, far = head_far(kept, near)
    cotangent_all = wide_rest(cotangent, cot_y, cot_x, cot_far)
    kept, far, cotangent_all = barrier(kept, far, cotangent_all)
    residual = source + kept + far.astype(F32)

    inverse_two = norm_scale(residual)
    normed_two = (residual * inverse_two * gain_two).astype(BF)
    near_y, near_x = barrier(*wide_near(normed_two))
    far_y, far_x = wide_far(near_y, near_x)
    trio = jnp.concatenate([normed_two, near_y, near_x], axis=0)
    early = jnp.concatenate([trio, flip(trio, "head", 1), trio[: 2 * own_rows]], axis=0)
    far_y, far_x, early = barrier(far_y, far_x, early)
    far = jnp.concatenate([far_y, far_x], axis=1)
    normed_two_all = lax.dynamic_update_slice_in_dim(
        early, jnp.concatenate([far, flip(far, "head", 1)], axis=0), 6 * own_rows, 0
    )
    gate_lin = simple_product(normed_two_all, gate_full)
    gate_lin, normed_two_all, up_down_full = barrier(gate_lin, normed_two_all, up_down_full)
    half = up_down_full.shape[1] // 2
    up_full, down_full = up_down_full[:, :half], up_down_full[:, half:]
    up_lin = simple_product(normed_two_all, up_full)
    sigmoid_gate = jax.nn.sigmoid(gate_lin)
    silu_gate = gate_lin * sigmoid_gate
    hidden = (silu_gate * up_lin).astype(BF)
    down_part = outer_sum(cotangent_all, hidden).astype(BF)
    down_sum = group_sum(down_part)
    hidden_grad = simple_product(after(cotangent_all, down_part), down_full)
    gate_act_grad = (
        hidden_grad * up_lin * sigmoid_gate * (1.0 + gate_lin * (1.0 - sigmoid_gate))
    ).astype(BF)
    up_act_grad = (hidden_grad * silu_gate).astype(BF)

    back = WideSum(
        (times_rows(gate_act_grad, gate_full) + times_rows(up_act_grad, up_full)).astype(BF)
    )
    gate_act_grad, up_act_grad, hidden = join([back], gate_act_grad, up_act_grad, hidden)
    sent = back.go_far()
    gate_part = outer_sum(normed_two_all, after(gate_act_grad, *sent)).astype(BF)
    hidden, up_act_grad, gate_part = join([back], hidden, up_act_grad, gate_part)
    gate_sum = group_sum(gate_part)
    sent = back.go_near()
    up_part = outer_sum(normed_two_all, after(up_act_grad, *sent)).astype(BF)
    hidden, up_part = join([back], hidden, up_part)
    up_sum = group_sum(up_part)
    normed_two_grad = back.total()
    residual_grad = cotangent.astype(F32) + norm_back(
        residual, gain_two, inverse_two, normed_two_grad
    )
    branch_grad = residual_grad.astype(BF)
    branch_y = flip(branch_grad, "head", 2)
    layer_part = times_rows(after(hidden, branch_grad), down_full).astype(BF)
    mlp_gain_part = jnp.sum(after(normed_two_grad, branch_grad) * residual * inverse_two, axis=0)
    branch_y, mlp_gain_part, layer_part = barrier(branch_y, mlp_gain_part, layer_part)
    branch_all = head_all(*head_rest(branch_grad, branch_y))
    attn_grad = simple_product(branch_all, out_full).astype(BF)
    attn_grad, branch_all, layer_part = barrier(attn_grad, branch_all, layer_part)

    row_delta = jnp.stack(
        [
            jnp.sum(
                attn_grad[:, r * width : (r + 1) * width].astype(F32)
                * attn_full[:, r * width : (r + 1) * width],
                axis=1,
            )
            for r in range(repeats)
        ]
    ).reshape(repeats, 1, rows)
    query_rot_grad, pair_grad = attend_back(
        kind,
        queries,
        pairs_full,
        attn_grad,
        low[None, :],
        high[None, :],
        index.reshape(blocks, rows, 1),
        lse.reshape(repeats, 1, rows),
        row_delta,
        repeats,
        width,
    )
    layer = WideSum(layer_part)
    query_rot_grad, pair_grad = join([layer], query_rot_grad, pair_grad)
    pair_sum = RingSum(pair_grad)
    sent = pair_sum.go()
    layer.go_far()
    out_part = outer_sum(branch_all, after(attn_low, *sent)).astype(BF)
    out_sum = lax.psum_scatter(out_part, "blk", scatter_dimension=0, tiled=True)
    down_mine, down_other = send_half(down_sum)
    out_part, down_mine, down_other = join([pair_sum, layer], out_part, down_mine, down_other)
    sent = pair_sum.go()
    layer.go_near()
    query_lin_grad = apply_rotary(
        after(query_rot_grad, *sent) * score_scale, table, -1.0
    ).astype(BF)
    down_grad = narrow_half(after(down_mine, *sent), down_other).T
    gate_mine, gate_other = send_half(gate_sum)
    query_lin_grad, down_grad, gate_mine, gate_other = join(
        [pair_sum, layer], query_lin_grad, down_grad, gate_mine, gate_other
    )
    sent = pair_sum.go()
    layer_out = (residual + layer.total()).astype(BF)
    gate_grad = narrow_half(after(gate_mine, *sent), gate_other)
    layer_out, gate_grad = join([pair_sum], layer_out, gate_grad)
    pair_sum.rest()
    pair_sum.go()
    up_mine, up_other = join([pair_sum], *send_half(up_sum))
    pair_total = pair_sum.total()
    pair_lin_grad = jnp.concatenate(
        [apply_rotary(pair_total[:, :width], table, -1.0), pair_total[:, width:]], axis=1
    ).astype(BF)
    lin_grad = jnp.concatenate([query_lin_grad, pair_lin_grad], axis=1)
    qkv_sum = RingSum(outer_sum(normed_all, lin_grad).astype(BF))
    sent = qkv_sum.go()
    lin_grad = after(lin_grad, *sent)
    normed_grad_part = times_rows(lin_grad, qkv_full)
    gain_part = jnp.sum(normed_grad_part * source_all * inverse_all, axis=0)
    kept, near = head_near(normed_grad_part)
    gain_grads = jnp.stack([gain_part, mlp_gain_part])
    gain_grads = gain_grads + flip(gain_grads, "head", 1)
    kept, near, gain_grads = join([qkv_sum], kept, near, gain_grads)
    qkv_sum.go()
    kept, far = head_far(kept, near)
    gain_grads = gain_grads + flip(gain_grads, "head", 2)
    kept, far, gain_grads, out_sum = join([qkv_sum], kept, far, gain_grads, out_sum)
    qkv_sum.go()
    bit = blocks // 2
    gain_grads = gain_back(gain_grads, bit)
    normed_grad = kept + far.astype(F32)
    tokens_grad = residual_grad + norm_back(source, gain_one, inverse_one, normed_grad)
    out_grad = out_sum.astype(F32).T
    gain_grads, tokens_grad, out_grad = join([qkv_sum], gain_grads, tokens_grad, out_grad)
    qkv_sum.rest()
    qkv_sum.go()
    while bit > 1:
        bit //= 2
        gain_grads = gain_back(gain_grads, bit)
    up_grad = narrow_half(up_mine, up_other)
    join([qkv_sum])
    qkv_grad = qkv_sum.total()
    return (
        layer_out,
        tokens_grad,
        gain_grads[0],
        qkv_grad[:, :query_cols],
        qkv_grad[:, query_cols : query_cols + width],
        qkv_grad[:, query_cols + width :],
        out_grad,
        gain_grads[1],
        gate_grad,
        up_grad,
        down_grad,
    )


def solution(mesh):
    return jax.shard_map(
        local,
        mesh=mesh,
        in_specs=(
            P(("blk", "head"), None),
            P("blk"),
            P("blk", "head"),
            P("blk", "head"),
            P("blk", "head"),
            P("head", "blk"),
            P("blk"),
            P("blk", "head"),
            P("blk", "head"),
            P("head", "blk"),
            P(),
            P(),
            P(("blk", "head"), None),
        ),
        out_specs=(
            P(("blk", "head"), None),
            P(("blk", "head"), None),
            P("blk"),
            P("blk", "head"),
            P("blk", "head"),
            P("blk", "head"),
            P("head", "blk"),
            P("blk"),
            P("blk", "head"),
            P("blk", "head"),
            P("head", "blk"),
        ),
        check_vma=False,
    )
```
